512 devices in a mesh: dp: 32 (over z, core), ctx: 16 (over x, y).
Axes of the slice: x: 4, y: 4, z: 16, core: 2. Of those that a mesh axis runs over, the one named last changes fastest.
Arguments:
- queries: bfloat16 [32, 2048, 2048], P('dp', 'ctx'), may hold values from -6 to 6
- key_vectors: bfloat16 [32, 2048, 2048], P('dp', 'ctx'), may hold values from -6 to 6
- values: bfloat16 [32, 2048, 2048], P('dp', 'ctx'), may hold values from -60 to 60
- grad_out: bfloat16 [32, 2048, 2048], P('dp', 'ctx'), may hold values from -40 to 40
- log_decay: float32 [32, 8, 2048], P('dp', None, 'ctx'), may hold values from -1 to 0, as said below
- norm_gain: float32 [2048], replicated, may hold values from 0.1 to 1.9
Outputs:
- grad_queries: bfloat16 [32, 2048, 2048], P('dp', 'ctx')
- grad_keys: bfloat16 [32, 2048, 2048], P('dp', 'ctx')
- grad_values: bfloat16 [32, 2048, 2048], P('dp', 'ctx')
- grad_gain: float32 [2048], replicated
The draws below stay inside these ranges and needn't reach their ends.
Inputs may be any that keep to these rules, and one draw needn't show every extreme that they name: log_decay is never positive.
All inputs are finite; a program needn't handle non-finite values.
Results may differ from the reference program's by a relative error of at most 0.029.
Values may be sent and summed in bfloat16 or wider, within the bound.
No kernel may reach another device: no remote copies, remote signals or barrier semaphores. Data moves between devices by JAX's collectives and lax.ppermute only.
A program may use at most 64 MiB of HBM per device.

```python
import math
import jax
import jax.numpy as jnp
from jax import lax

HEADS = 8
KD = 256
VD = 256
TOK_DEV = 128
BATCH = 32
SEQUENCE_LENGTH = 2048


def draw_log_decay(key, part):
    key = jax.random.fold_in(key, 11)
    keys = jax.random.split(key, 10)
    order_key, quick_key, middle_key, gradual_key, block_key = (keys[0], keys[1], keys[2], keys[3], keys[4])
    jitter_key, spike_key, depth_key, place_key, steep_key = (keys[5], keys[6], keys[7], keys[8], keys[9])
    quick_edge = 0.125
    middle_edge = 0.375
    steep_edge = 0.5
    ranking = jax.random.permutation(order_key, HEADS)
    share = (ranking.astype(jnp.float32) + 0.5) / HEADS
    fast_rate = jnp.exp(jax.random.uniform(quick_key, (HEADS,), minval=math.log(1.0 / 50.0), maxval=math.log(1.0 / 30.0)))
    middle_rate = jnp.exp(jax.random.uniform(middle_key, (HEADS,), minval=math.log(0.6), maxval=math.log(0.9))) / TOK_DEV
    slow_rate = jnp.exp(jax.random.uniform(gradual_key, (HEADS,), minval=math.log(0.1), maxval=math.log(0.4))) / SEQUENCE_LENGTH
    level = jnp.where(share < quick_edge, fast_rate, jnp.where(share < middle_edge, middle_rate, slow_rate))
    blocks = SEQUENCE_LENGTH // TOK_DEV
    multiplier = jnp.exp(jax.random.uniform(block_key, (BATCH, HEADS, blocks), minval=math.log(0.6), maxval=math.log(1.5)))
    multiplier = jnp.repeat(multiplier, TOK_DEV, axis=2)
    tensor_dimensions = (BATCH, HEADS, SEQUENCE_LENGTH)
    jitter_amplitude = jax.random.uniform(jitter_key, tensor_dimensions, minval=0.5, maxval=1.5)
    spike_positions = jax.random.uniform(spike_key, tensor_dimensions) < 3.0 / SEQUENCE_LENGTH
    spike_depth = jax.random.uniform(depth_key, tensor_dimensions, minval=0.2, maxval=0.5)
    spike_decay_loss = jnp.where(spike_positions, jnp.log(1.0 - spike_depth), 0.0)
    steep_head = jnp.logical_and(share >= middle_edge, share < steep_edge)
    lowest_block = max(1, blocks // 2)
    highest_block = max(lowest_block + 1, blocks - 1)
    steep_block = jax.random.randint(place_key, (BATCH, HEADS), lowest_block, highest_block)
    steep_end = (steep_block + 1) * TOK_DEV
    places = jnp.arange(SEQUENCE_LENGTH, dtype=jnp.int32)
    inside = jnp.logical_and(places[None, None, :] >= steep_end[:, :, None] - 8, places[None, None, :] < steep_end[:, :, None])
    inside = jnp.logical_and(inside, steep_head[None, :, None])
    steep_rate = jax.random.uniform(steep_key, tensor_dimensions, minval=0.58, maxval=0.65)
    steep_loss = jnp.where(inside, steep_rate, 0.0)
    total = -level[None, :, None] * multiplier * jitter_amplitude + spike_decay_loss - steep_loss
    return jnp.maximum(total, -1.0).astype(jnp.float32)


def draw_values(key, part):
    key = jax.random.fold_in(key, 12)
    base_key, row_key, column_key = jax.random.split(key, 3)
    tensor_dimensions = (BATCH, SEQUENCE_LENGTH, HEADS * VD)
    reference_level = jnp.clip(jax.random.normal(base_key, tensor_dimensions), -6.0, 6.0)
    row_scale = jnp.exp(jax.random.uniform(row_key, (BATCH, SEQUENCE_LENGTH, 1), minval=math.log(0.3), maxval=math.log(3.0)))
    column_scale = jnp.exp(jax.random.uniform(column_key, (HEADS * VD,), minval=math.log(0.3), maxval=math.log(3.0)))
    return (reference_level * row_scale * column_scale).astype(jnp.bfloat16)


def draw_grad_out(key, part):
    key = jax.random.fold_in(key, 13)
    base_key, row_key = jax.random.split(key, 2)
    tensor_dimensions = (BATCH, SEQUENCE_LENGTH, HEADS * VD)
    reference_level = jnp.clip(jax.random.normal(base_key, tensor_dimensions), -6.0, 6.0)
    positions = jnp.arange(SEQUENCE_LENGTH, dtype=jnp.float32) / SEQUENCE_LENGTH
    sequence_scale = jnp.arange(BATCH, dtype=jnp.float32) / BATCH
    trend_scale = (1.0 + 2.0 * positions)[None, :, None] * (1.0 + 2.0 * sequence_scale)[:, None, None]
    row_scale = jnp.exp(jax.random.uniform(row_key, (BATCH, SEQUENCE_LENGTH, 1), minval=math.log(0.5), maxval=math.log(2.0)))
    return (0.3 * reference_level * trend_scale * row_scale).astype(jnp.bfloat16)


def steps_of(own_key, extent, shards, smallest, top_value):
    gain, own = 1.0, jax.random.fold_in(own_key, 6)
    for dim, blocks in shards:
        heights = jnp.exp(jax.random.uniform(jax.random.fold_in(own, dim), (blocks,), jnp.float32, smallest / len(shards), top_value / len(shards)))
        gain = gain * jnp.repeat(heights, extent[dim] // blocks).reshape([-1 if axis == dim else 1 for axis in range(len(extent))])
    return gain


def bell_draw(key, extent, width, most, cuts=(), kind=jnp.bfloat16):
    loudness = steps_of(key, extent, cuts, -0.22, 0.18) if cuts else 1.0
    drawn = jax.random.normal(key, extent, jnp.float32) * width * loudness
    return jnp.minimum(jnp.maximum(drawn, -most), most).astype(kind)


def setup_inputs(seed: int = 0) -> dict:
    key_list = jax.random.split(jax.random.key(seed), 7)
    queries = bell_draw(key_list[0], (BATCH, SEQUENCE_LENGTH, HEADS * KD), 1.0, 6.0, ((0, 32), (1, 16)))
    key_vectors = bell_draw(key_list[1], (BATCH, SEQUENCE_LENGTH, HEADS * KD), 1.0, 6.0, ((0, 32), (1, 16)))
    values = draw_values(jax.random.fold_in(key_list[6], 71), 0)
    grad_out = draw_grad_out(jax.random.fold_in(key_list[6], 71), 0)
    log_decay = draw_log_decay(jax.random.fold_in(key_list[6], 71), 0)
    norm_gain = jnp.clip(1.0 + 0.18 * jax.random.normal(key_list[5], (HEADS * VD,), jnp.float32), 0.1, 1.9)
    return dict(queries=queries, key_vectors=key_vectors, values=values, grad_out=grad_out, log_decay=log_decay, norm_gain=norm_gain)


EPSILON = 1e-05

def carry_step(carried, item):
    summed, block_state = item
    updated = jnp.exp(summed.astype(jnp.float32))[:, None, None] * carried.astype(jnp.float32) + block_state.astype(jnp.float32)
    return (updated.astype(jnp.bfloat16), carried)

def sequence_grads(queries, key_vectors, values, grad_out, log_decay, norm_gain):
    blocks = SEQUENCE_LENGTH // TOK_DEV
    scaling = KD ** (-0.5)
    query_heads = queries.reshape(blocks, TOK_DEV, HEADS, KD).astype(jnp.float32)
    key_heads = key_vectors.reshape(blocks, TOK_DEV, HEADS, KD).astype(jnp.float32)
    value_heads = values.reshape(blocks, TOK_DEV, HEADS, VD).astype(jnp.float32)
    out_heads = grad_out.reshape(blocks, TOK_DEV, HEADS, VD).astype(jnp.float32)
    gain_heads = norm_gain.reshape(HEADS, VD)
    decay = log_decay.reshape(HEADS, blocks, TOK_DEV).transpose(1, 0, 2)
    cumulative = jnp.cumsum(decay, axis=2)
    block_end = cumulative[:, :, -1]
    position = jnp.arange(TOK_DEV)
    causal = position[:, None] >= position[None, :]
    weight = jnp.where(causal, jnp.exp(jnp.minimum(cumulative[..., :, None] - cumulative[..., None, :], 0.0)), 0.0)
    scores = jnp.einsum('nthk,nshk->nhts', query_heads, key_heads)
    retained = (scores * scaling * weight).astype(jnp.bfloat16).astype(jnp.float32)
    to_end = jnp.exp(block_end[:, :, None] - cumulative).transpose(0, 2, 1)[..., None]
    key_tail = (key_heads * to_end).astype(jnp.bfloat16).astype(jnp.float32)
    block_state = jnp.einsum('nshk,nshv->nhkv', key_tail, value_heads).astype(jnp.bfloat16)
    block_total = block_end.astype(jnp.bfloat16)
    start_state = jnp.zeros((HEADS, KD, VD), jnp.bfloat16)
    _, state_in = lax.scan(carry_step, start_state, (block_total, block_state))
    state_wide = state_in.astype(jnp.float32)
    from_start = (scaling * jnp.exp(cumulative)).transpose(0, 2, 1)[..., None]
    query_tail = (query_heads * from_start).astype(jnp.bfloat16).astype(jnp.float32)
    output = jnp.einsum('nhts,nshv->nthv', retained, value_heads) + jnp.einsum('nthk,nhkv->nthv', query_tail, state_wide)
    centred = output - lax.optimization_barrier(jnp.mean(output, axis=-1, keepdims=True))
    inverse = lax.rsqrt(lax.optimization_barrier(jnp.mean(centred * centred, axis=-1, keepdims=True)) + EPSILON)
    normed = centred * inverse
    gain_part = lax.optimization_barrier(jnp.sum(out_heads * normed, axis=(0, 1)))
    scaled_grad = out_heads * gain_heads
    grad_o = inverse * (scaled_grad - lax.optimization_barrier(jnp.mean(scaled_grad, axis=-1, keepdims=True)) - normed * lax.optimization_barrier(jnp.mean(scaled_grad * normed, axis=-1, keepdims=True)))
    grad_o = grad_o.astype(jnp.bfloat16).astype(jnp.float32)
    grad_scores = jnp.einsum('nthv,nshv->nhts', grad_o, value_heads)
    grad_retained = (grad_scores * scaling * weight).astype(jnp.bfloat16).astype(jnp.float32)
    local_queries = jnp.einsum('nhts,nshk->nthk', grad_retained, key_heads)
    local_keys = jnp.einsum('nhts,nthk->nshk', grad_retained, query_heads)
    local_values = jnp.einsum('nhts,nthv->nshv', retained, grad_o)
    block_grad = jnp.einsum('nthk,nthv->nhkv', query_tail, grad_o).astype(jnp.bfloat16)
    _, grad_in = lax.scan(carry_step, start_state, (block_total, block_grad), reverse=True)
    grad_wide = grad_in.astype(jnp.float32)
    cross_queries = jnp.einsum('nthv,nhkv->nthk', grad_o, state_wide) * from_start
    cross_keys = jnp.einsum('nshv,nhkv->nshk', value_heads, grad_wide) * to_end
    cross_values = jnp.einsum('nshk,nhkv->nshv', key_heads, grad_wide) * to_end
    grad_queries = (local_queries + cross_queries).astype(jnp.bfloat16).reshape(SEQUENCE_LENGTH, HEADS * KD)
    grad_keys = (local_keys + cross_keys).astype(jnp.bfloat16).reshape(SEQUENCE_LENGTH, HEADS * KD)
    grad_values = (local_values + cross_values).astype(jnp.bfloat16).reshape(SEQUENCE_LENGTH, HEADS * VD)
    return (grad_queries, grad_keys, grad_values, gain_part)

def reference(queries, key_vectors, values, grad_out, log_decay, norm_gain):

    def per_sequence(item):
        return sequence_grads(item[0], item[1], item[2], item[3], item[4], norm_gain)
    grad_queries, grad_keys, grad_values, gain_parts = lax.map(per_sequence, (queries, key_vectors, values, grad_out, log_decay))
    grad_gain = (lax.optimization_barrier(jnp.sum(gain_parts, axis=0)) / BATCH).reshape(HEADS * VD)
    return (grad_queries, grad_keys, grad_values, grad_gain)
```

```python
import functools

import jax
import jax.numpy as jnp
from jax import lax
from jax.experimental import pallas as pl
from jax.experimental.pallas import tpu as pltpu
from jax.sharding import PartitionSpec as P

HEADS = 8
KD = 256
VD = 256
EPSILON = 1e-05

TOK = 128
GROUP = 8
CHUNK = 256
CHUNKS = GROUP * TOK // CHUNK
ROWS = 4 * TOK + 16
BACK = 3 * TOK

F32 = jnp.float32
BF16 = jnp.bfloat16
SCALE = KD ** (-0.5)


def nn(a, b):
    return lax.dot_general(a, b, (((1,), (0,)), ((), ())), preferred_element_type=F32)


def nt(a, b):
    return lax.dot_general(a, b, (((1,), (1,)), ((), ())), preferred_element_type=F32)


def tn(a, b):
    return lax.dot_general(a, b, (((0,), (0,)), ((), ())), preferred_element_type=F32)


def call(kernel, outs, scratch=(), smem=()):
    def run(*args):
        specs = [
            pl.BlockSpec(memory_space=pltpu.SMEM if i in smem else pltpu.VMEM)
            for i in range(len(args))
        ]
        return pl.pallas_call(
            kernel,
            out_shape=[jax.ShapeDtypeStruct(shape, kind) for shape, kind in outs],
            in_specs=specs,
            out_specs=[pl.BlockSpec(memory_space=pltpu.VMEM) for _ in outs],
            scratch_shapes=list(scratch),
            compiler_params=pltpu.CompilerParams(vmem_limit_bytes=24 * 1024 * 1024),
        )(*args)

    return run


def pack_kernel(q_ref, k_ref, v_ref, g_ref, decay_ref, out_ref):
    row = lax.broadcasted_iota(jnp.int32, (16, 256), 0)
    for h in range(HEADS):
        cols = slice(h * KD, (h + 1) * KD)
        for n, ref in enumerate((q_ref, k_ref, v_ref, g_ref)):
            out_ref[h, n * TOK : (n + 1) * TOK, :] = ref[:, cols]
        decay = decay_ref[h : h + 1, :]
        high = decay.astype(BF16).astype(F32)
        rest = decay - high
        middle = rest.astype(BF16).astype(F32)
        low = rest - middle
        first = jnp.concatenate([high, middle], axis=1)
        second = jnp.concatenate([low, jnp.zeros_like(low)], axis=1)
        pieces = jnp.where(row == 0, first, jnp.where(row == 1, second, 0.0))
        out_ref[h, 4 * TOK :, :] = pieces.astype(BF16)


def part(ref, c, n):
    per = CHUNK // TOK
    return ref[c * per : (c + 1) * per, n * TOK : (n + 1) * TOK, :].reshape(CHUNK, 256)


def chunk_decay(col_ref, row_ref, c):
    column = col_ref[:, c : c + 1]
    line = row_ref[c : c + 1, :]
    return column, line, line[:, CHUNK - 1 :]


def chunk_weight(column, line):
    t = lax.broadcasted_iota(jnp.int32, (CHUNK, CHUNK), 0)
    s = lax.broadcasted_iota(jnp.int32, (CHUNK, CHUNK), 1)
    return jnp.where(t >= s, jnp.exp(jnp.minimum(column - line, 0.0)), 0.0)


def state_kernel(got_ref, total_ref, states_ref, col_ref, row_ref, decay_ref):
    decay_ref[...] = jnp.zeros_like(decay_ref)
    for i in range(GROUP):
        pieces = got_ref[i, 4 * TOK :, :].astype(F32)
        decay = pieces[0:1, :TOK] + pieces[0:1, TOK:] + pieces[1:2, :TOK]
        c, j = divmod(i * TOK, CHUNK)
        decay_ref[c : c + 1, j : j + TOK] = decay
    decay = decay_ref[...]
    t = lax.broadcasted_iota(jnp.int32, (CHUNK, CHUNK), 0)
    s = lax.broadcasted_iota(jnp.int32, (CHUNK, CHUNK), 1)
    lower = (t >= s).astype(F32)
    exact = dict(precision=lax.Precision.HIGHEST, preferred_element_type=F32)
    row_ref[...] = lax.dot_general(decay, lower, (((1,), (1,)), ((), ())), **exact)
    col_ref[...] = lax.dot_general(lower, decay, (((1,), (1,)), ((), ())), **exact)
    carried = jnp.zeros((KD, VD), F32)
    for c in range(CHUNKS):
        states_ref[c] = carried
        column, line, last = chunk_decay(col_ref, row_ref, c)
        key_tail = (part(got_ref, c, 1).astype(F32) * jnp.exp(last - column)).astype(BF16)
        carried = jnp.exp(last) * carried + tn(key_tail, part(got_ref, c, 2))
    total_ref[...] = carried.astype(BF16)


def local_kernel(got_ref, states_ref, col_ref, row_ref, retained_ref, output_ref):
    for c in range(CHUNKS):
        column, line, last = chunk_decay(col_ref, row_ref, c)
        q = part(got_ref, c, 0)
        scores = nt(q, part(got_ref, c, 1))
        retained = (scores * (SCALE * chunk_weight(column, line))).astype(BF16)
        retained_ref[c] = retained
        output = nn(retained, part(got_ref, c, 2))
        if c:
            tail = (q.astype(F32) * (SCALE * jnp.exp(column))).astype(BF16)
            output = output + nn(tail, states_ref[c].astype(BF16))
        output_ref[c] = output


def output_kernel(
    half_ref, got_ref, states_ref, output_ref, middle_ref, col_ref, row_ref, gain_ref,
    grad_ref, state_in_ref, state_grads_ref, total_ref, gain_part_ref, block_grads,
):
    gain = gain_ref[0:1, :]
    middle = jnp.where(half_ref[0] > 0, middle_ref[...].astype(F32), 0.0)
    middle_low = middle.astype(BF16)
    before = jnp.zeros((1, 1), F32)
    gain_part = jnp.zeros((1, VD), F32)
    for c in range(CHUNKS):
        column, line, last = chunk_decay(col_ref, row_ref, c)
        q = part(got_ref, c, 0).astype(F32)
        tail = (q * (SCALE * jnp.exp(column))).astype(BF16)
        state_in_ref[c] = (states_ref[c] + jnp.exp(before) * middle).astype(BF16)
        output = output_ref[c] + jnp.exp(before) * nn(tail, middle_low)
        before = before + last
        centred = output - jnp.mean(output, axis=1, keepdims=True)
        inverse = lax.rsqrt(jnp.mean(centred * centred, axis=1, keepdims=True) + EPSILON)
        normed = centred * inverse
        wide = part(got_ref, c, 3).astype(F32)
        gain_part = gain_part + jnp.sum(wide * normed, axis=0, keepdims=True)
        scaled = wide * gain
        grad = inverse * (
            scaled
            - jnp.mean(scaled, axis=1, keepdims=True)
            - normed * jnp.mean(scaled * normed, axis=1, keepdims=True)
        )
        grad = grad.astype(BF16)
        grad_ref[c] = grad
        block_grads[c] = tn(tail, grad)
    carried = jnp.zeros((KD, VD), F32)
    for c in reversed(range(CHUNKS)):
        state_grads_ref[c] = carried.astype(BF16)
        _, _, last = chunk_decay(col_ref, row_ref, c)
        carried = jnp.exp(last) * carried + block_grads[c]
    total_ref[...] = carried.astype(BF16)
    first = lax.broadcasted_iota(jnp.int32, (8, VD), 0) == 0
    gain_part_ref[...] = jnp.where(first, gain_part, 0.0)


def grads_kernel(
    got_ref, grad_ref, retained_ref, state_in_ref, state_grads_ref, col_ref, row_ref,
    queries_ref, keys_ref, values_ref,
):
    for c in range(CHUNKS):
        column, line, last = chunk_decay(col_ref, row_ref, c)
        q, k, v = part(got_ref, c, 0), part(got_ref, c, 1), part(got_ref, c, 2)
        grad = grad_ref[c]
        scores = nt(grad, v)
        grad_retained = (scores * (SCALE * chunk_weight(column, line))).astype(BF16)
        from_start = SCALE * jnp.exp(column)
        queries = nn(grad_retained, k) + from_start * nt(grad, state_in_ref[c])
        queries_ref[c] = queries.astype(BF16)
        keys = tn(grad_retained, q)
        values = tn(retained_ref[c], grad)
        if c < CHUNKS - 1:
            to_end = jnp.exp(last - column)
            keys = keys + to_end * nt(v, state_grads_ref[c])
            values = values + to_end * nn(k, state_grads_ref[c])
        keys_ref[c] = keys
        values_ref[c] = values


def last_kernel(
    half_ref, got_ref, queries_ref, keys_ref, values_ref, middle_ref, col_ref, row_ref, out_ref
):
    middle = jnp.where(half_ref[0] > 0, 0.0, middle_ref[...].astype(F32)).astype(BF16)
    after = jnp.zeros((1, 1), F32)
    for c in reversed(range(CHUNKS)):
        column, line, last = chunk_decay(col_ref, row_ref, c)
        to_end = jnp.exp(after + (last - column))
        after = after + last
        k, v = part(got_ref, c, 1), part(got_ref, c, 2)
        keys = keys_ref[c] + to_end * nt(v, middle)
        values = values_ref[c] + to_end * nn(k, middle)
        per = CHUNK // TOK
        for n, item in enumerate((queries_ref[c], keys.astype(BF16), values.astype(BF16))):
            out_ref[c * per : (c + 1) * per, n * TOK : (n + 1) * TOK, :] = item.reshape(per, TOK, 256)


def unpack_kernel(got_ref, queries_ref, keys_ref, values_ref):
    for h in range(HEADS):
        cols = slice(h * KD, (h + 1) * KD)
        for n, ref in enumerate((queries_ref, keys_ref, values_ref)):
            ref[:, cols] = got_ref[h, n * TOK : (n + 1) * TOK, :]


def sum_over_dp(value):
    size = lax.axis_size("dp")

    def fetch(item, step):
        return lax.ppermute(item, "dp", [(i, i ^ step) for i in range(size)])

    step = 1
    while step < size:
        if step * 4 <= size:
            one, two, three = fetch(value, step), fetch(value, 2 * step), fetch(value, 3 * step)
            value = (value + one) + (two + three)
            step *= 4
        else:
            value = value + fetch(value, step)
            step *= 2
    return value


def shards(queries, key_vectors, values, grad_out, log_decay, norm_gain):
    place = lax.axis_index("ctx")
    blocks = lax.axis_size("ctx")
    halves = [list(range(GROUP)), list(range(GROUP, 2 * GROUP))]
    swap = [(i, i ^ GROUP) for i in range(blocks)]
    half = (place // GROUP).astype(jnp.int32).reshape(1)
    gain = lax.dynamic_slice_in_dim(norm_gain.reshape(HEADS, VD), place % GROUP, 1, 0)
    square = (CHUNKS, CHUNK, 256)

    packed = call(pack_kernel, [((GROUP, ROWS, 256), BF16)])(
        queries[0], key_vectors[0], values[0], grad_out[0], log_decay[0]
    )[0]
    got = lax.all_to_all(packed, "ctx", 0, 0, axis_index_groups=halves, tiled=True)
    total, states, column, line = call(
        state_kernel,
        [((KD, VD), BF16), ((CHUNKS, KD, VD), F32), ((CHUNK, 8), F32), ((8, CHUNK), F32)],
        [pltpu.VMEM((8, CHUNK), F32)],
    )(got)
    middle = lax.ppermute(total, "ctx", swap)
    retained, output = call(local_kernel, [(square, BF16), (square, F32)])(
        got, states, column, line
    )
    grad, state_in, state_grads, total_grad, gain_part = call(
        output_kernel,
        [(square, BF16), (square, BF16), (square, BF16), ((KD, VD), BF16), ((8, VD), F32)],
        [pltpu.VMEM((CHUNKS, KD, VD), F32)],
        smem=(0,),
    )(half, got, states, output, middle, column, line, gain)
    middle_grad = lax.ppermute(total_grad, "ctx", swap)
    gains = lax.all_to_all(
        jnp.broadcast_to(gain_part[None], (blocks, 8, VD)), "ctx", 0, 0, tiled=True
    )
    gain_sum = sum_over_dp(gains[:GROUP, 0] + gains[GROUP:, 0])
    grad_queries, grad_keys, grad_values = call(
        grads_kernel, [(square, BF16), (square, F32), (square, F32)]
    )(got, grad, retained, state_in, state_grads, column, line)
    back = call(last_kernel, [((GROUP, BACK, 256), BF16)], smem=(0,))(
        half, got, grad_queries, grad_keys, grad_values, middle_grad, column, line
    )[0]
    back = lax.all_to_all(back, "ctx", 0, 0, axis_index_groups=halves, tiled=True)
    results = call(unpack_kernel, [((TOK, HEADS * KD), BF16)] * 3)(back)
    grad_gain = (gain_sum / lax.axis_size("dp")).reshape(HEADS * VD)
    return (*(item[None] for item in results), grad_gain)


def solution(mesh):
    return jax.shard_map(
        shards,
        mesh=mesh,
        in_specs=(
            P("dp", "ctx", None),
            P("dp", "ctx", None),
            P("dp", "ctx", None),
            P("dp", "ctx", None),
            P("dp", None, "ctx"),
            P(),
        ),
        out_specs=(P("dp", "ctx", None), P("dp", "ctx", None), P("dp", "ctx", None), P()),
        check_vma=False,
    )
```

```python
import jax
import jax.numpy as jnp
from jax import lax
from jax.experimental import pallas as pl
from jax.experimental.pallas import tpu as pltpu
from jax.sharding import PartitionSpec as P

HEADS = 8
KD = 256
VD = 256
EPSILON = 1e-05

TOK = 128
GROUP = 8
CHUNK = 256
CHUNKS = GROUP * TOK // CHUNK
ROWS = 4 * TOK + 16
BACK = 3 * TOK

F32 = jnp.float32
BF16 = jnp.bfloat16
SCALE = KD ** (-0.5)


def nn(a, b):
    return lax.dot_general(a, b, (((1,), (0,)), ((), ())), preferred_element_type=F32)


def nt(a, b):
    return lax.dot_general(a, b, (((1,), (1,)), ((), ())), preferred_element_type=F32)


def tn(a, b):
    return lax.dot_general(a, b, (((0,), (0,)), ((), ())), preferred_element_type=F32)


def call(kernel, outs, scratch=(), places=None, out_place=None, grant=16):
    def run(*args):
        where = places or {}
        return pl.pallas_call(
            kernel,
            out_shape=[jax.ShapeDtypeStruct(shape, kind) for shape, kind in outs],
            in_specs=[
                pl.BlockSpec(memory_space=where.get(i, pltpu.VMEM)) for i in range(len(args))
            ],
            out_specs=[pl.BlockSpec(memory_space=out_place or pltpu.VMEM) for _ in outs],
            scratch_shapes=list(scratch),
            compiler_params=pltpu.CompilerParams(vmem_limit_bytes=grant * 1024 * 1024),
        )(*args)

    return run


def pack_kernel(q_ref, k_ref, v_ref, g_ref, decay_ref, out_ref, decay_buf, sems, decay_sem):
    fetch = pltpu.make_async_copy(decay_ref, decay_buf, decay_sem)
    fetch.start()
    copies = []
    for n, ref in enumerate((q_ref, k_ref, v_ref, g_ref)):
        for h in range(HEADS):
            copies.append(
                pltpu.make_async_copy(
                    ref.at[:, h * KD : (h + 1) * KD],
                    out_ref.at[h, n * TOK : (n + 1) * TOK, :],
                    sems.at[n * HEADS + h],
                )
            )
    for copy in copies:
        copy.start()
    fetch.wait()
    row = lax.broadcasted_iota(jnp.int32, (16, 256), 0)
    for h in range(HEADS):
        decay = decay_buf[h : h + 1, :]
        high = decay.astype(BF16).astype(F32)
        rest = decay - high
        middle = rest.astype(BF16).astype(F32)
        low = rest - middle
        first = jnp.concatenate([high, middle], axis=1)
        second = jnp.concatenate([low, jnp.zeros_like(low)], axis=1)
        pieces = jnp.where(row == 0, first, jnp.where(row == 1, second, 0.0))
        out_ref[h, 4 * TOK :, :] = pieces.astype(BF16)
    for copy in copies:
        copy.wait()


def part(ref, c, n):
    per = CHUNK // TOK
    return ref[c * per : (c + 1) * per, n * TOK : (n + 1) * TOK, :].reshape(CHUNK, 256)


def chunk_decay(col_ref, row_ref, c):
    column = col_ref[:, c : c + 1]
    line = row_ref[c : c + 1, :]
    return column, line, line[:, CHUNK - 1 :]


def chunk_weight(column, line):
    t = lax.broadcasted_iota(jnp.int32, (CHUNK, CHUNK), 0)
    s = lax.broadcasted_iota(jnp.int32, (CHUNK, CHUNK), 1)
    return jnp.where(t >= s, jnp.exp(jnp.minimum(column - line, 0.0)), 0.0)


def state_kernel(got_ref, total_ref, states_ref, col_ref, row_ref, decay_ref):
    decay_ref[...] = jnp.zeros_like(decay_ref)
    for i in range(GROUP):
        pieces = got_ref[i, 4 * TOK :, :].astype(F32)
        decay = pieces[0:1, :TOK] + pieces[0:1, TOK:] + pieces[1:2, :TOK]
        c, j = divmod(i * TOK, CHUNK)
        decay_ref[c : c + 1, j : j + TOK] = decay
    decay = decay_ref[...]
    t = lax.broadcasted_iota(jnp.int32, (CHUNK, CHUNK), 0)
    s = lax.broadcasted_iota(jnp.int32, (CHUNK, CHUNK), 1)
    lower = (t >= s).astype(F32)
    exact = dict(precision=lax.Precision.HIGHEST, preferred_element_type=F32)
    row_ref[...] = lax.dot_general(decay, lower, (((1,), (1,)), ((), ())), **exact)
    col_ref[...] = lax.dot_general(lower, decay, (((1,), (1,)), ((), ())), **exact)
    carried = jnp.zeros((KD, VD), F32)
    for c in range(CHUNKS):
        states_ref[c] = carried
        column, line, last = chunk_decay(col_ref, row_ref, c)
        key_tail = (part(got_ref, c, 1).astype(F32) * jnp.exp(last - column)).astype(BF16)
        carried = jnp.exp(last) * carried + tn(key_tail, part(got_ref, c, 2))
    total_ref[...] = carried.astype(BF16)


def local_kernel(got_ref, states_ref, col_ref, row_ref, retained_ref, output_ref):
    for c in range(CHUNKS):
        column, line, last = chunk_decay(col_ref, row_ref, c)
        q = part(got_ref, c, 0)
        scores = nt(q, part(got_ref, c, 1))
        retained = (scores * (SCALE * chunk_weight(column, line))).astype(BF16)
        retained_ref[c] = retained
        output = nn(retained, part(got_ref, c, 2))
        if c:
            tail = (q.astype(F32) * (SCALE * jnp.exp(column))).astype(BF16)
            output = output + nn(tail, states_ref[c].astype(BF16))
        output_ref[c] = output


def output_kernel(
    where_ref, got_ref, states_ref, retained_ref, output_ref, middle_ref, col_ref, row_ref, gain_ref,
    queries_ref, keys_ref, values_ref, total_ref, gain_part_ref, block_grads,
):
    gain = gain_ref[0:1, :]
    middle = jnp.where(where_ref[0] > 0, middle_ref[...].astype(F32), 0.0)
    middle_low = middle.astype(BF16)
    before = jnp.zeros((1, 1), F32)
    gain_part = jnp.zeros((1, VD), F32)
    for c in range(CHUNKS):
        column, line, last = chunk_decay(col_ref, row_ref, c)
        q, k, v = part(got_ref, c, 0), part(got_ref, c, 1), part(got_ref, c, 2)
        from_start = SCALE * jnp.exp(column)
        tail = (q.astype(F32) * from_start).astype(BF16)
        state_in = (states_ref[c] + jnp.exp(before) * middle).astype(BF16)
        output = output_ref[c] + jnp.exp(before) * nn(tail, middle_low)
        before = before + last
        centred = output - jnp.mean(output, axis=1, keepdims=True)
        inverse = lax.rsqrt(jnp.mean(centred * centred, axis=1, keepdims=True) + EPSILON)
        normed = centred * inverse
        wide = part(got_ref, c, 3).astype(F32)
        gain_part = gain_part + jnp.sum(wide * normed, axis=0, keepdims=True)
        scaled = wide * gain
        grad = inverse * (
            scaled
            - jnp.mean(scaled, axis=1, keepdims=True)
            - normed * jnp.mean(scaled * normed, axis=1, keepdims=True)
        )
        grad = grad.astype(BF16)
        block_grads[c] = tn(tail, grad)
        scores = nt(grad, v)
        grad_retained = (scores * (SCALE * chunk_weight(column, line))).astype(BF16)
        queries = nn(grad_retained, k) + from_start * nt(grad, state_in)
        queries_ref[c] = queries.astype(BF16)
        keys_ref[c] = tn(grad_retained, q)
        values_ref[c] = tn(retained_ref[c], grad)
    carried = jnp.zeros((KD, VD), F32)
    for c in reversed(range(CHUNKS)):
        column, _, last = chunk_decay(col_ref, row_ref, c)
        if c < CHUNKS - 1:
            to_end = jnp.exp(last - column)
            after = carried.astype(BF16)
            keys_ref[c] += to_end * nt(part(got_ref, c, 2), after)
            values_ref[c] += to_end * nn(part(got_ref, c, 1), after)
        carried = jnp.exp(last) * carried + block_grads[c]
    total_ref[...] = carried.astype(BF16)
    mine = lax.broadcasted_iota(jnp.int32, (HEADS, VD), 0) == where_ref[1]
    gain_part_ref[...] = jnp.where(mine, gain_part, 0.0)


def last_kernel(
    where_ref, got_ref, queries_ref, keys_ref, values_ref, middle_ref, col_ref, row_ref,
    out_ref, out_buf, sems,
):
    middle = jnp.where(where_ref[0] > 0, 0.0, middle_ref[...].astype(F32)).astype(BF16)
    after = jnp.zeros((1, 1), F32)
    per = CHUNK // TOK
    copies = []
    for c in reversed(range(CHUNKS)):
        column, line, last = chunk_decay(col_ref, row_ref, c)
        to_end = jnp.exp(after + (last - column))
        after = after + last
        k, v = part(got_ref, c, 1), part(got_ref, c, 2)
        keys = keys_ref[c] + to_end * nt(v, middle)
        values = values_ref[c] + to_end * nn(k, middle)
        blocks = slice(c * per, (c + 1) * per)
        for n, item in enumerate((queries_ref[c], keys.astype(BF16), values.astype(BF16))):
            out_buf[blocks, n * TOK : (n + 1) * TOK, :] = item.reshape(per, TOK, 256)
        copies.append(pltpu.make_async_copy(out_buf.at[blocks], out_ref.at[blocks], sems.at[c]))
        copies[-1].start()
    for copy in copies:
        copy.wait()


def unpack_kernel(got_ref, queries_ref, keys_ref, values_ref, sems):
    copies = []
    for n, ref in enumerate((queries_ref, keys_ref, values_ref)):
        for h in range(HEADS):
            copies.append(
                pltpu.make_async_copy(
                    got_ref.at[h, n * TOK : (n + 1) * TOK, :],
                    ref.at[:, h * KD : (h + 1) * KD],
                    sems.at[n * HEADS + h],
                )
            )
    for copy in copies:
        copy.start()
    for copy in copies:
        copy.wait()


def shards(queries, key_vectors, values, grad_out, log_decay, norm_gain):
    place = lax.axis_index("ctx")
    blocks = lax.axis_size("ctx")
    halves = [list(range(GROUP)), list(range(GROUP, 2 * GROUP))]
    swap = [(i, i ^ GROUP) for i in range(blocks)]
    where = jnp.stack([place // GROUP, place % GROUP]).astype(jnp.int32)
    gain = lax.dynamic_slice_in_dim(norm_gain.reshape(HEADS, VD), place % GROUP, 1, 0)
    square = (CHUNKS, CHUNK, 256)

    packed = call(
        pack_kernel,
        [((GROUP, ROWS, 256), BF16)],
        [
            pltpu.VMEM((HEADS, TOK), F32),
            pltpu.SemaphoreType.DMA((4 * HEADS,)),
            pltpu.SemaphoreType.DMA,
        ],
        places={i: pltpu.HBM for i in range(5)},
        grant=56,
    )(queries[0], key_vectors[0], values[0], grad_out[0], log_decay[0])[0]
    got = lax.all_to_all(packed, "ctx", 0, 0, axis_index_groups=halves, tiled=True)
    total, states, column, line = call(
        state_kernel,
        [((KD, VD), BF16), ((CHUNKS, KD, VD), F32), ((CHUNK, 8), F32), ((8, CHUNK), F32)],
        [pltpu.VMEM((8, CHUNK), F32)],
    )(got)
    middle = lax.ppermute(total, "ctx", swap)
    retained, output = call(local_kernel, [(square, BF16), (square, F32)])(
        got, states, column, line
    )
    grad_queries, grad_keys, grad_values, total_grad, gain_part = call(
        output_kernel,
        [(square, BF16), (square, F32), (square, F32), ((KD, VD), BF16), ((HEADS, VD), F32)],
        [pltpu.VMEM((CHUNKS, KD, VD), F32)],
        places={0: pltpu.SMEM},
    )(where, got, states, retained, output, middle, column, line, gain)
    middle_grad = lax.ppermute(total_grad, "ctx", swap)
    gains = lax.all_to_all(
        jnp.broadcast_to(gain_part[None], (blocks, HEADS, VD)), "ctx", 0, 0, tiled=True
    )
    back = call(
        last_kernel,
        [((GROUP, BACK, 256), BF16)],
        [pltpu.VMEM((GROUP, BACK, 256), BF16), pltpu.SemaphoreType.DMA((CHUNKS,))],
        places={0: pltpu.SMEM},
        out_place=pltpu.HBM,
    )(where, got, grad_queries, grad_keys, grad_values, middle_grad, column, line)[0]
    back = lax.all_to_all(back, "ctx", 0, 0, axis_index_groups=halves, tiled=True)
    gain_all = lax.all_gather(jnp.sum(gains, axis=0), "dp")
    results = call(
        unpack_kernel,
        [((TOK, HEADS * KD), BF16)] * 3,
        [pltpu.SemaphoreType.DMA((3 * HEADS,))],
        places={0: pl.ANY},
        out_place=pltpu.HBM,
    )(back)
    grad_gain = (jnp.sum(gain_all, axis=0) / lax.axis_size("dp")).reshape(HEADS * VD)
    return (*(item[None] for item in results), grad_gain)


def solution(mesh):
    return jax.shard_map(
        shards,
        mesh=mesh,
        in_specs=(
            P("dp", "ctx", None),
            P("dp", "ctx", None),
            P("dp", "ctx", None),
            P("dp", "ctx", None),
            P("dp", None, "ctx"),
            P(),
        ),
        out_specs=(P("dp", "ctx", None), P("dp", "ctx", None), P("dp", "ctx", None), P()),
        check_vma=False,
    )
```

```python
import jax
import jax.numpy as jnp
from jax import lax
from jax.experimental import pallas as pl
from jax.experimental.pallas import tpu as pltpu
from jax.sharding import PartitionSpec as P

HEADS = 8
KD = 256
VD = 256
EPSILON = 1e-05

TOK = 128
GROUP = 8
CHUNK = 256
CHUNKS = GROUP * TOK // CHUNK
ROWS = 4 * TOK + 16
BACK = 3 * TOK

F32 = jnp.float32
BF16 = jnp.bfloat16
SCALE = KD ** (-0.5)


def nn(a, b):
    return lax.dot_general(a, b, (((1,), (0,)), ((), ())), preferred_element_type=F32)


def nt(a, b):
    return lax.dot_general(a, b, (((1,), (1,)), ((), ())), preferred_element_type=F32)


def tn(a, b):
    return lax.dot_general(a, b, (((0,), (0,)), ((), ())), preferred_element_type=F32)


def call(kernel, outs, scratch=(), places=None, far=(), grant=16):
    def run(*args):
        where = places or {}
        args = [
            pltpu.with_memory_space_constraint(item, pltpu.HBM) if where.get(i) == pltpu.HBM else item
            for i, item in enumerate(args)
        ]
        return pl.pallas_call(
            kernel,
            out_shape=[
                (pltpu.HBM if i in far else jax.ShapeDtypeStruct)(shape, kind)
                for i, (shape, kind) in enumerate(outs)
            ],
            in_specs=[
                pl.BlockSpec(memory_space=where.get(i, pltpu.VMEM)) for i in range(len(args))
            ],
            out_specs=[
                pl.BlockSpec(memory_space=pltpu.HBM if i in far else pltpu.VMEM)
                for i in range(len(outs))
            ],
            scratch_shapes=list(scratch),
            compiler_params=pltpu.CompilerParams(vmem_limit_bytes=grant * 1024 * 1024),
        )(*args)

    return run


def pack_kernel(
    q_ref, k_ref, v_ref, g_ref, decay_ref, out_ref, decay_buf, pieces_buf, sems, decay_sem, pieces_sem
):
    fetch = pltpu.make_async_copy(decay_ref, decay_buf, decay_sem)
    fetch.start()
    copies = []
    for n, ref in enumerate((q_ref, k_ref, v_ref, g_ref)):
        for h in range(HEADS):
            copies.append(
                pltpu.make_async_copy(
                    ref.at[:, h * KD : (h + 1) * KD],
                    out_ref.at[h, n * TOK : (n + 1) * TOK, :],
                    sems.at[n * HEADS + h],
                )
            )
    for copy in copies:
        copy.start()
    fetch.wait()
    row = lax.broadcasted_iota(jnp.int32, (16, 256), 0)
    for h in range(HEADS):
        decay = decay_buf[h : h + 1, :]
        high = decay.astype(BF16).astype(F32)
        rest = decay - high
        middle = rest.astype(BF16).astype(F32)
        low = rest - middle
        first = jnp.concatenate([high, middle], axis=1)
        second = jnp.concatenate([low, jnp.zeros_like(low)], axis=1)
        pieces = jnp.where(row == 0, first, jnp.where(row == 1, second, 0.0))
        pieces_buf[h] = pieces.astype(BF16)
    store = pltpu.make_async_copy(pieces_buf, out_ref.at[:, 4 * TOK :, :], pieces_sem)
    store.start()
    for copy in copies:
        copy.wait()
    store.wait()


def part(ref, c, n):
    per = CHUNK // TOK
    return ref[c * per : (c + 1) * per, n * TOK : (n + 1) * TOK, :].reshape(CHUNK, 256)


def put(ref, c, n, item):
    per = CHUNK // TOK
    item = item.astype(BF16).reshape(per, TOK, 256)
    ref[c * per : (c + 1) * per, n * TOK : (n + 1) * TOK, :] = item


def rows_of(ref, c, n):
    per = CHUNK // TOK
    return ref.at[c * per : (c + 1) * per, n * TOK : (n + 1) * TOK, :]


def send(source, target, sems, c, n):
    copy = pltpu.make_async_copy(rows_of(source, c, n), rows_of(target, c, n), sems.at[n, c])
    copy.start()
    return copy


def chunk_decay(col_ref, row_ref, c):
    column = col_ref[:, c : c + 1]
    line = row_ref[c : c + 1, :]
    return column, line, line[:, CHUNK - 1 :]


def chunk_weight(column, line):
    t = lax.broadcasted_iota(jnp.int32, (CHUNK, CHUNK), 0)
    s = lax.broadcasted_iota(jnp.int32, (CHUNK, CHUNK), 1)
    return jnp.where(t >= s, jnp.exp(jnp.minimum(column - line, 0.0)), 0.0)


def state_kernel(got_ref, total_ref, states_ref, col_ref, row_ref, decay_ref):
    decay_ref[...] = jnp.zeros_like(decay_ref)
    for i in range(GROUP):
        pieces = got_ref[i, 4 * TOK :, :].astype(F32)
        decay = pieces[0:1, :TOK] + pieces[0:1, TOK:] + pieces[1:2, :TOK]
        c, j = divmod(i * TOK, CHUNK)
        decay_ref[c : c + 1, j : j + TOK] = decay
    decay = decay_ref[...]
    t = lax.broadcasted_iota(jnp.int32, (CHUNK, CHUNK), 0)
    s = lax.broadcasted_iota(jnp.int32, (CHUNK, CHUNK), 1)
    lower = (t >= s).astype(F32)
    exact = dict(precision=lax.Precision.HIGHEST, preferred_element_type=F32)
    row_ref[...] = lax.dot_general(decay, lower, (((1,), (1,)), ((), ())), **exact)
    col_ref[...] = lax.dot_general(lower, decay, (((1,), (1,)), ((), ())), **exact)
    carried = jnp.zeros((KD, VD), F32)
    for c in range(CHUNKS):
        states_ref[c] = carried
        column, line, last = chunk_decay(col_ref, row_ref, c)
        key_tail = (part(got_ref, c, 1).astype(F32) * jnp.exp(last - column)).astype(BF16)
        carried = jnp.exp(last) * carried + tn(key_tail, part(got_ref, c, 2))
    total_ref[...] = carried.astype(BF16)


def local_kernel(got_ref, states_ref, col_ref, row_ref, retained_ref, output_ref):
    for c in range(CHUNKS):
        column, line, last = chunk_decay(col_ref, row_ref, c)
        q = part(got_ref, c, 0)
        scores = nt(q, part(got_ref, c, 1))
        retained = (scores * (SCALE * chunk_weight(column, line))).astype(BF16)
        retained_ref[c] = retained
        output = nn(retained, part(got_ref, c, 2))
        if c:
            tail = (q.astype(F32) * (SCALE * jnp.exp(column))).astype(BF16)
            output = output + nn(tail, states_ref[c].astype(BF16))
        output_ref[c] = output


def output_kernel(
    where_ref, got_ref, states_ref, retained_ref, output_ref, middle_ref, col_ref, row_ref, gain_ref,
    out_ref, total_ref, gain_part_ref, back_ref, total_buf, block_grads, keys_acc, values_acc, sems,
):
    copies = []
    gain = gain_ref[0:1, :]
    middle = jnp.where(where_ref[0] > 0, middle_ref[...].astype(F32), 0.0)
    middle_low = middle.astype(BF16)
    before = jnp.zeros((1, 1), F32)
    gain_part = jnp.zeros((1, VD), F32)
    for c in range(CHUNKS):
        column, line, last = chunk_decay(col_ref, row_ref, c)
        q, k, v = part(got_ref, c, 0), part(got_ref, c, 1), part(got_ref, c, 2)
        from_start = SCALE * jnp.exp(column)
        tail = (q.astype(F32) * from_start).astype(BF16)
        state_in = (states_ref[c] + jnp.exp(before) * middle).astype(BF16)
        output = output_ref[c] + jnp.exp(before) * nn(tail, middle_low)
        before = before + last
        centred = output - jnp.mean(output, axis=1, keepdims=True)
        inverse = lax.rsqrt(jnp.mean(centred * centred, axis=1, keepdims=True) + EPSILON)
        normed = centred * inverse
        wide = part(got_ref, c, 3).astype(F32)
        gain_part = gain_part + jnp.sum(wide * normed, axis=0, keepdims=True)
        scaled = wide * gain
        grad = inverse * (
            scaled
            - jnp.mean(scaled, axis=1, keepdims=True)
            - normed * jnp.mean(scaled * normed, axis=1, keepdims=True)
        )
        grad = grad.astype(BF16)
        block_grads[c] = tn(tail, grad)
        scores = nt(grad, v)
        grad_retained = (scores * (SCALE * chunk_weight(column, line))).astype(BF16)
        queries = nn(grad_retained, k) + from_start * nt(grad, state_in)
        put(back_ref, c, 0, queries)
        copies.append(send(back_ref, out_ref, sems, c, 0))
        keys_acc[c] = tn(grad_retained, q)
        values_acc[c] = tn(retained_ref[c], grad)
    carried = jnp.zeros((KD, VD), F32)
    for c in reversed(range(CHUNKS)):
        column, _, last = chunk_decay(col_ref, row_ref, c)
        keys, values = keys_acc[c], values_acc[c]
        if c < CHUNKS - 1:
            to_end = jnp.exp(last - column)
            after = carried.astype(BF16)
            keys = keys + to_end * nt(part(got_ref, c, 2), after)
            values = values + to_end * nn(part(got_ref, c, 1), after)
        put(back_ref, c, 1, keys)
        put(back_ref, c, 2, values)
        copies.append(send(back_ref, out_ref, sems, c, 1))
        copies.append(send(back_ref, out_ref, sems, c, 2))
        carried = jnp.exp(last) * carried + block_grads[c]
    total_buf[...] = carried.astype(BF16)
    copies.append(pltpu.make_async_copy(total_buf, total_ref, sems.at[3, 0]))
    copies[-1].start()
    mine = lax.broadcasted_iota(jnp.int32, (HEADS, VD), 0) == where_ref[1]
    gain_part_ref[...] = jnp.where(mine, gain_part, 0.0)
    for copy in copies:
        copy.wait()


def last_kernel(where_ref, got_ref, back_ref, middle_ref, col_ref, row_ref, out_ref, buf, sems, out_sems):
    fetches = {}
    for c in reversed(range(CHUNKS)):
        for n in range(3):
            fetches[c, n] = send(back_ref, buf, sems, c, n)
    middle = jnp.where(where_ref[0] > 0, 0.0, middle_ref[...].astype(F32)).astype(BF16)
    after = jnp.zeros((1, 1), F32)
    copies = []
    for c in reversed(range(CHUNKS)):
        column, line, last = chunk_decay(col_ref, row_ref, c)
        to_end = jnp.exp(after + (last - column))
        after = after + last
        k, v = part(got_ref, c, 1), part(got_ref, c, 2)
        keys, values = to_end * nt(v, middle), to_end * nn(k, middle)
        for n in range(3):
            fetches[c, n].wait()
        put(buf, c, 1, part(buf, c, 1).astype(F32) + keys)
        put(buf, c, 2, part(buf, c, 2).astype(F32) + values)
        for n in range(3):
            copies.append(send(buf, out_ref, out_sems, c, n))
    for copy in copies:
        copy.wait()


def unpack_kernel(got_ref, queries_ref, keys_ref, values_ref, sems):
    copies = []
    for n, ref in enumerate((queries_ref, keys_ref, values_ref)):
        for h in range(HEADS):
            copies.append(
                pltpu.make_async_copy(
                    got_ref.at[h, n * TOK : (n + 1) * TOK, :],
                    ref.at[:, h * KD : (h + 1) * KD],
                    sems.at[n * HEADS + h],
                )
            )
    for copy in copies:
        copy.start()
    for copy in copies:
        copy.wait()


def shards(queries, key_vectors, values, grad_out, log_decay, norm_gain):
    place = lax.axis_index("ctx")
    blocks = lax.axis_size("ctx")
    halves = [list(range(GROUP)), list(range(GROUP, 2 * GROUP))]
    size = lax.axis_size("dp")
    planes = [list(range(2 * i * blocks, 2 * (i + 1) * blocks)) for i in range(size // 2)]
    columns = [list(range(core, size, 2)) for core in range(2)]
    swap = [(i, i ^ GROUP) for i in range(blocks)]
    where = jnp.stack([place // GROUP, place % GROUP]).astype(jnp.int32)
    gain = lax.dynamic_slice_in_dim(norm_gain.reshape(HEADS, VD), place % GROUP, 1, 0)
    square = (CHUNKS, CHUNK, 256)

    packed = call(
        pack_kernel,
        [((GROUP, ROWS, 256), BF16)],
        [
            pltpu.VMEM((HEADS, TOK), F32),
            pltpu.VMEM((HEADS, 16, 256), BF16),
            pltpu.SemaphoreType.DMA((4 * HEADS,)),
            pltpu.SemaphoreType.DMA,
            pltpu.SemaphoreType.DMA,
        ],
        places={i: pltpu.HBM for i in range(5)},
        far=(0,),
    )(queries[0], key_vectors[0], values[0], grad_out[0], log_decay[0])[0]
    got = lax.all_to_all(packed, "ctx", 0, 0, axis_index_groups=halves, tiled=True)
    total, states, column, line = call(
        state_kernel,
        [((KD, VD), BF16), ((CHUNKS, KD, VD), F32), ((CHUNK, 8), F32), ((8, CHUNK), F32)],
        [pltpu.VMEM((8, CHUNK), F32)],
    )(got)
    middle = lax.ppermute(total, "ctx", swap)
    retained, output = call(local_kernel, [(square, BF16), (square, F32)])(
        got, states, column, line
    )
    back, total_grad, gain_part = call(
        output_kernel,
        [((GROUP, BACK, 256), BF16), ((KD, VD), BF16), ((HEADS, VD), F32)],
        [
            pltpu.VMEM((GROUP, BACK, 256), BF16),
            pltpu.VMEM((KD, VD), BF16),
            *[pltpu.VMEM((CHUNKS, 256, 256), F32)] * 3,
            pltpu.SemaphoreType.DMA((4, CHUNKS)),
        ],
        places={0: pltpu.SMEM},
        far=(0, 1),
    )(where, got, states, retained, output, middle, column, line, gain)
    middle_grad = lax.ppermute(total_grad, "ctx", swap)
    gains = lax.all_to_all(
        jnp.broadcast_to(gain_part[None], (2 * blocks, HEADS, VD)),
        ("dp", "ctx"), 0, 0, axis_index_groups=planes, tiled=True,
    )
    back = call(
        last_kernel,
        [((GROUP, BACK, 256), BF16)],
        [pltpu.VMEM((GROUP, BACK, 256), BF16), *[pltpu.SemaphoreType.DMA((3, CHUNKS))] * 2],
        places={0: pltpu.SMEM, 2: pltpu.HBM},
        far=(0,),
    )(where, got, back, middle_grad, column, line)[0]
    back = lax.all_to_all(back, "ctx", 0, 0, axis_index_groups=halves, tiled=True)
    gain_all = lax.all_gather(jnp.sum(gains, axis=0), "dp", axis_index_groups=columns)
    results = call(
        unpack_kernel,
        [((TOK, HEADS * KD), BF16)] * 3,
        [pltpu.SemaphoreType.DMA((3 * HEADS,))],
        places={0: pl.ANY},
        far=(0, 1, 2),
    )(back)
    grad_gain = (jnp.sum(gain_all, axis=0) / size).reshape(HEADS * VD)
    return (*(item[None] for item in results), grad_gain)


def solution(mesh):
    return jax.shard_map(
        shards,
        mesh=mesh,
        in_specs=(
            P("dp", "ctx", None),
            P("dp", "ctx", None),
            P("dp", "ctx", None),
            P("dp", "ctx", None),
            P("dp", None, "ctx"),
            P(),
        ),
        out_specs=(P("dp", "ctx", None), P("dp", "ctx", None), P("dp", "ctx", None), P()),
        check_vma=False,
    )
```

```python
import jax
import jax.numpy as jnp
from jax import lax
from jax.experimental import pallas as pl
from jax.experimental.pallas import tpu as pltpu
from jax.sharding import PartitionSpec as P

HEADS = 8
KD = 256
VD = 256
EPSILON = 1e-05

TOK = 128
GROUP = 8
CHUNK = 256
CHUNKS = GROUP * TOK // CHUNK
ROWS = 4 * TOK + 16
BACK = 3 * TOK

F32 = jnp.float32
BF16 = jnp.bfloat16
SCALE = KD ** (-0.5)


def nn(a, b):
    return lax.dot_general(a, b, (((1,), (0,)), ((), ())), preferred_element_type=F32)


def nt(a, b):
    return lax.dot_general(a, b, (((1,), (1,)), ((), ())), preferred_element_type=F32)


def tn(a, b):
    return lax.dot_general(a, b, (((0,), (0,)), ((), ())), preferred_element_type=F32)


def call(kernel, outs, scratch=(), places=None, far=(), cost=None, aliases=None):
    def run(*args):
        where = places or {}
        args = [
            pltpu.with_memory_space_constraint(item, pltpu.HBM) if where.get(i) == pltpu.HBM else item
            for i, item in enumerate(args)
        ]
        return pl.pallas_call(
            kernel,
            out_shape=[
                (pltpu.HBM if i in far else jax.ShapeDtypeStruct)(shape, kind)
                for i, (shape, kind) in enumerate(outs)
            ],
            in_specs=[
                pl.BlockSpec(memory_space=where.get(i, pltpu.VMEM)) for i in range(len(args))
            ],
            out_specs=[
                pl.BlockSpec(memory_space=pltpu.HBM if i in far else pltpu.VMEM)
                for i in range(len(outs))
            ],
            scratch_shapes=list(scratch),
            compiler_params=pltpu.CompilerParams(vmem_limit_bytes=16 * 1024 * 1024),
            cost_estimate=cost and pl.CostEstimate(flops=cost[0], bytes_accessed=cost[1], transcendentals=0),
            input_output_aliases=aliases or {},
        )(*args)

    return run


def pack_kernel(
    q_ref, k_ref, v_ref, g_ref, decay_ref, out_ref, buf, decay_buf, sems, decay_sem, out_sems
):
    fetch = pltpu.make_async_copy(decay_ref, decay_buf, decay_sem)
    fetch.start()
    copies = [
        [
            pltpu.make_async_copy(
                ref.at[:, h * KD : (h + 1) * KD],
                buf.at[h, n * TOK : (n + 1) * TOK, :],
                sems.at[h, n],
            )
            for n, ref in enumerate((q_ref, k_ref, v_ref, g_ref))
        ]
        for h in range(HEADS)
    ]
    for copy in sum(copies, []):
        copy.start()
    fetch.wait()
    row = lax.broadcasted_iota(jnp.int32, (16, 256), 0)
    for h in range(HEADS):
        decay = decay_buf[h : h + 1, :]
        high = decay.astype(BF16).astype(F32)
        rest = decay - high
        middle = rest.astype(BF16).astype(F32)
        low = rest - middle
        first = jnp.concatenate([high, middle], axis=1)
        second = jnp.concatenate([low, jnp.zeros_like(low)], axis=1)
        pieces = jnp.where(row == 0, first, jnp.where(row == 1, second, 0.0))
        buf[h, 4 * TOK :, :] = pieces.astype(BF16)
    stores = []
    for h in range(HEADS):
        for copy in copies[h]:
            copy.wait()
        stores.append(pltpu.make_async_copy(buf.at[h], out_ref.at[h], out_sems.at[h]))
        stores[-1].start()
    for store in stores:
        store.wait()


def part(ref, c, n):
    per = CHUNK // TOK
    return ref[c * per : (c + 1) * per, n * TOK : (n + 1) * TOK, :].reshape(CHUNK, 256)


def put(ref, c, n, item):
    per = CHUNK // TOK
    item = item.astype(BF16).reshape(per, TOK, 256)
    ref[c * per : (c + 1) * per, n * TOK : (n + 1) * TOK, :] = item


def rows_of(ref, c, n):
    per = CHUNK // TOK
    return ref.at[c * per : (c + 1) * per, n * TOK : (n + 1) * TOK, :]


def send(source, target, sems, c, n):
    copy = pltpu.make_async_copy(rows_of(source, c, n), rows_of(target, c, n), sems.at[n, c])
    copy.start()
    return copy


def chunk_decay(col_ref, row_ref, c):
    column = col_ref[:, c : c + 1]
    line = row_ref[c : c + 1, :]
    return column, line, line[:, CHUNK - 1 :]


def chunk_weight(column, line):
    t = lax.broadcasted_iota(jnp.int32, (CHUNK, CHUNK), 0)
    s = lax.broadcasted_iota(jnp.int32, (CHUNK, CHUNK), 1)
    return jnp.where(t >= s, jnp.exp(jnp.minimum(column - line, 0.0)), 0.0)


def state_kernel(got_ref, total_ref, states_ref, col_ref, row_ref, decay_ref):
    decay_ref[...] = jnp.zeros_like(decay_ref)
    for i in range(GROUP):
        pieces = got_ref[i, 4 * TOK :, :].astype(F32)
        decay = pieces[0:1, :TOK] + pieces[0:1, TOK:] + pieces[1:2, :TOK]
        c, j = divmod(i * TOK, CHUNK)
        decay_ref[c : c + 1, j : j + TOK] = decay
    decay = decay_ref[...]
    t = lax.broadcasted_iota(jnp.int32, (CHUNK, CHUNK), 0)
    s = lax.broadcasted_iota(jnp.int32, (CHUNK, CHUNK), 1)
    lower = (t >= s).astype(F32)
    exact = dict(precision=lax.Precision.HIGHEST, preferred_element_type=F32)
    row_ref[...] = lax.dot_general(decay, lower, (((1,), (1,)), ((), ())), **exact)
    col_ref[...] = lax.dot_general(lower, decay, (((1,), (1,)), ((), ())), **exact)
    carried = jnp.zeros((KD, VD), F32)
    for c in range(CHUNKS):
        states_ref[c] = carried
        column, line, last = chunk_decay(col_ref, row_ref, c)
        key_tail = (part(got_ref, c, 1).astype(F32) * jnp.exp(last - column)).astype(BF16)
        carried = jnp.exp(last) * carried + tn(key_tail, part(got_ref, c, 2))
    total_ref[...] = carried.astype(BF16)


def local_kernel(got_ref, states_ref, col_ref, row_ref, retained_ref, output_ref):
    for c in range(CHUNKS):
        column, line, last = chunk_decay(col_ref, row_ref, c)
        q = part(got_ref, c, 0)
        scores = nt(q, part(got_ref, c, 1))
        retained = (scores * (SCALE * chunk_weight(column, line))).astype(BF16)
        retained_ref[c] = retained
        output = nn(retained, part(got_ref, c, 2))
        if c:
            tail = (q.astype(F32) * (SCALE * jnp.exp(column))).astype(BF16)
            output = output + nn(tail, states_ref[c].astype(BF16))
        output_ref[c] = output


def output_kernel(
    where_ref, got_ref, states_ref, retained_ref, output_ref, middle_ref, col_ref, row_ref, gain_ref,
    out_ref, total_ref, gain_part_ref, back_ref, total_buf, block_grads, keys_acc, values_acc, sems,
):
    copies = []
    gain = gain_ref[0:1, :]
    middle = jnp.where(where_ref[0] > 0, middle_ref[...].astype(F32), 0.0)
    middle_low = middle.astype(BF16)
    before = jnp.zeros((1, 1), F32)
    gain_part = jnp.zeros((1, VD), F32)
    for c in range(CHUNKS):
        column, line, last = chunk_decay(col_ref, row_ref, c)
        q, k, v = part(got_ref, c, 0), part(got_ref, c, 1), part(got_ref, c, 2)
        from_start = SCALE * jnp.exp(column)
        tail = (q.astype(F32) * from_start).astype(BF16)
        state_in = (states_ref[c] + jnp.exp(before) * middle).astype(BF16)
        output = output_ref[c] + jnp.exp(before) * nn(tail, middle_low)
        before = before + last
        centred = output - jnp.mean(output, axis=1, keepdims=True)
        inverse = lax.rsqrt(jnp.mean(centred * centred, axis=1, keepdims=True) + EPSILON)
        normed = centred * inverse
        wide = part(got_ref, c, 3).astype(F32)
        gain_part = gain_part + jnp.sum(wide * normed, axis=0, keepdims=True)
        scaled = wide * gain
        grad = inverse * (
            scaled
            - jnp.mean(scaled, axis=1, keepdims=True)
            - normed * jnp.mean(scaled * normed, axis=1, keepdims=True)
        )
        grad = grad.astype(BF16)
        block_grads[c] = tn(tail, grad)
        scores = nt(grad, v)
        grad_retained = (scores * (SCALE * chunk_weight(column, line))).astype(BF16)
        queries = nn(grad_retained, k) + from_start * nt(grad, state_in)
        put(back_ref, c, 0, queries)
        copies.append(send(back_ref, out_ref, sems, c, 0))
        keys_acc[c] = tn(grad_retained, q)
        values_acc[c] = tn(retained_ref[c], grad)
    carried = jnp.zeros((KD, VD), F32)
    for c in reversed(range(CHUNKS)):
        column, _, last = chunk_decay(col_ref, row_ref, c)
        keys, values = keys_acc[c], values_acc[c]
        if c < CHUNKS - 1:
            to_end = jnp.exp(last - column)
            after = carried.astype(BF16)
            keys = keys + to_end * nt(part(got_ref, c, 2), after)
            values = values + to_end * nn(part(got_ref, c, 1), after)
        put(back_ref, c, 1, keys)
        put(back_ref, c, 2, values)
        copies.append(send(back_ref, out_ref, sems, c, 1))
        copies.append(send(back_ref, out_ref, sems, c, 2))
        carried = jnp.exp(last) * carried + block_grads[c]
    total_buf[...] = carried.astype(BF16)
    copies.append(pltpu.make_async_copy(total_buf, total_ref, sems.at[3, 0]))
    copies[-1].start()
    mine = lax.broadcasted_iota(jnp.int32, (HEADS, VD), 0) == where_ref[1]
    gain_part_ref[...] = jnp.where(mine, gain_part, 0.0)
    for copy in copies:
        copy.wait()


def spread_kernel(gain_ref, out_ref):
    for i in range(out_ref.shape[0]):
        out_ref[i] = gain_ref[...]


def last_kernel(where_ref, got_ref, back_ref, middle_ref, col_ref, row_ref, out_ref, buf, sems, out_sems):
    fetches = {}
    for c in reversed(range(CHUNKS)):
        for n in (1, 2):
            fetches[c, n] = send(back_ref, buf, sems, c, n)
    middle = jnp.where(where_ref[0] > 0, 0.0, middle_ref[...].astype(F32)).astype(BF16)
    after = jnp.zeros((1, 1), F32)
    copies = []
    for c in reversed(range(CHUNKS)):
        column, line, last = chunk_decay(col_ref, row_ref, c)
        to_end = jnp.exp(after + (last - column))
        after = after + last
        keys = to_end * nt(part(got_ref, c, 2), middle)
        values = to_end * nn(part(got_ref, c, 1), middle)
        for n, item in ((1, keys), (2, values)):
            fetches[c, n].wait()
            put(buf, c, n, part(buf, c, n).astype(F32) + item)
            copies.append(send(buf, out_ref, out_sems, c, n))
    for copy in copies:
        copy.wait()


def unpack_kernel(got_ref, queries_ref, keys_ref, values_ref, sems):
    copies = []
    for n, ref in enumerate((queries_ref, keys_ref, values_ref)):
        for h in range(HEADS):
            copies.append(
                pltpu.make_async_copy(
                    got_ref.at[h, n * TOK : (n + 1) * TOK, :],
                    ref.at[:, h * KD : (h + 1) * KD],
                    sems.at[n * HEADS + h],
                )
            )
    for copy in copies:
        copy.start()
    for copy in copies:
        copy.wait()


def shards(queries, key_vectors, values, grad_out, log_decay, norm_gain):
    place = lax.axis_index("ctx")
    blocks = lax.axis_size("ctx")
    halves = [list(range(GROUP)), list(range(GROUP, 2 * GROUP))]
    size = lax.axis_size("dp")
    swap = [(i, i ^ GROUP) for i in range(blocks)]
    where = jnp.stack([place // GROUP, place % GROUP]).astype(jnp.int32)
    gain = lax.dynamic_slice_in_dim(norm_gain.reshape(HEADS, VD), place % GROUP, 1, 0)
    square = (CHUNKS, CHUNK, 256)

    packed = call(
        pack_kernel,
        [((GROUP, ROWS, 256), BF16)],
        [
            pltpu.VMEM((GROUP, ROWS, 256), BF16),
            pltpu.VMEM((HEADS, TOK), F32),
            pltpu.SemaphoreType.DMA((HEADS, 4)),
            pltpu.SemaphoreType.DMA,
            pltpu.SemaphoreType.DMA((HEADS,)),
        ],
        places={i: pltpu.HBM for i in range(5)},
        far=(0,),
    )(queries[0], key_vectors[0], values[0], grad_out[0], log_decay[0])[0]
    got = lax.all_to_all(packed, "ctx", 0, 0, axis_index_groups=halves, tiled=True)
    total, states, column, line = call(
        state_kernel,
        [((KD, VD), BF16), ((CHUNKS, KD, VD), F32), ((CHUNK, 8), F32), ((8, CHUNK), F32)],
        [pltpu.VMEM((8, CHUNK), F32)],
    )(got)
    middle = lax.ppermute(total, "ctx", swap)
    retained, output = call(local_kernel, [(square, BF16), (square, F32)])(
        got, states, column, line
    )
    back, total_grad, gain_part = call(
        output_kernel,
        [((GROUP, BACK, 256), BF16), ((KD, VD), BF16), ((HEADS, VD), F32)],
        [
            pltpu.VMEM((GROUP, BACK, 256), BF16),
            pltpu.VMEM((KD, VD), BF16),
            *[pltpu.VMEM((CHUNKS, 256, 256), F32)] * 3,
            pltpu.SemaphoreType.DMA((4, CHUNKS)),
        ],
        places={0: pltpu.SMEM},
        far=(0, 1),
    )(where, got, states, retained, output, middle, column, line, gain)
    middle_grad = lax.ppermute(total_grad, "ctx", swap)
    gains = lax.all_to_all(
        call(spread_kernel, [((blocks, HEADS, VD), F32)], cost=(4 * 10**9, 2**20))(gain_part)[0],
        "ctx", 0, 0, tiled=True,
    )
    back = call(
        last_kernel,
        [((GROUP, BACK, 256), BF16)],
        [pltpu.VMEM((GROUP, BACK, 256), BF16), *[pltpu.SemaphoreType.DMA((3, CHUNKS))] * 2],
        places={0: pltpu.SMEM, 2: pltpu.HBM},
        far=(0,),
        aliases={2: 0},
    )(where, got, back, middle_grad, column, line)[0]
    back = lax.all_to_all(back, "ctx", 0, 0, axis_index_groups=halves, tiled=True)
    gain_all = lax.all_gather(jnp.sum(gains, axis=0), "dp")
    results = call(
        unpack_kernel,
        [((TOK, HEADS * KD), BF16)] * 3,
        [pltpu.SemaphoreType.DMA((3 * HEADS,))],
        places={0: pl.ANY},
        far=(0, 1, 2),
    )(back)
    grad_gain = (jnp.sum(gain_all, axis=0) / size).reshape(HEADS * VD)
    return (*(item[None] for item in results), grad_gain)


def solution(mesh):
    return jax.shard_map(
        shards,
        mesh=mesh,
        in_specs=(
            P("dp", "ctx", None),
            P("dp", "ctx", None),
            P("dp", "ctx", None),
            P("dp", "ctx", None),
            P("dp", None, "ctx"),
            P(),
        ),
        out_specs=(P("dp", "ctx", None), P("dp", "ctx", None), P("dp", "ctx", None), P()),
        check_vma=False,
    )
```

```python
import jax
import jax.numpy as jnp
from jax import lax
from jax.experimental import pallas as pl
from jax.experimental.pallas import tpu as pltpu
from jax.sharding import PartitionSpec as P

HEADS = 8
KD = 256
VD = 256
EPSILON = 1e-05

TOK = 128
GROUP = 8
CHUNK = 256
CHUNKS = GROUP * TOK // CHUNK
ROWS = 4 * TOK + 16
BACK = 3 * TOK

F32 = jnp.float32
BF16 = jnp.bfloat16
SCALE = KD ** (-0.5)


def nn(a, b):
    return lax.dot_general(a, b, (((1,), (0,)), ((), ())), preferred_element_type=F32)


def nt(a, b):
    return lax.dot_general(a, b, (((1,), (1,)), ((), ())), preferred_element_type=F32)


def tn(a, b):
    return lax.dot_general(a, b, (((0,), (0,)), ((), ())), preferred_element_type=F32)


def call(kernel, outs, scratch=(), places=None, far=(), cost=None, aliases=None):
    def run(*args):
        where = places or {}
        args = [
            pltpu.with_memory_space_constraint(item, pltpu.HBM) if where.get(i) == pltpu.HBM else item
            for i, item in enumerate(args)
        ]
        return pl.pallas_call(
            kernel,
            out_shape=[
                (pltpu.HBM if i in far else jax.ShapeDtypeStruct)(shape, kind)
                for i, (shape, kind) in enumerate(outs)
            ],
            in_specs=[
                pl.BlockSpec(memory_space=where.get(i, pltpu.VMEM)) for i in range(len(args))
            ],
            out_specs=[
                pl.BlockSpec(memory_space=pltpu.HBM if i in far else pltpu.VMEM)
                for i in range(len(outs))
            ],
            scratch_shapes=list(scratch),
            compiler_params=pltpu.CompilerParams(vmem_limit_bytes=16 * 1024 * 1024),
            cost_estimate=cost and pl.CostEstimate(flops=cost[0], bytes_accessed=cost[1], transcendentals=0),
            input_output_aliases=aliases or {},
        )(*args)

    return run


def pack_kernel(
    q_ref, k_ref, v_ref, g_ref, decay_ref, out_ref, buf, decay_buf, sems, decay_sem, out_sems
):
    fetch = pltpu.make_async_copy(decay_ref, decay_buf, decay_sem)
    fetch.start()
    copies = [
        [
            pltpu.make_async_copy(
                ref.at[:, h * KD : (h + 1) * KD],
                buf.at[h, n * TOK : (n + 1) * TOK, :],
                sems.at[h, n],
            )
            for n, ref in enumerate((q_ref, k_ref, v_ref, g_ref))
        ]
        for h in range(HEADS)
    ]
    for copy in sum(copies, []):
        copy.start()
    fetch.wait()
    row = lax.broadcasted_iota(jnp.int32, (16, 256), 0)
    for h in range(HEADS):
        decay = decay_buf[h : h + 1, :]
        high = decay.astype(BF16).astype(F32)
        rest = decay - high
        middle = rest.astype(BF16).astype(F32)
        low = rest - middle
        first = jnp.concatenate([high, middle], axis=1)
        second = jnp.concatenate([low, jnp.zeros_like(low)], axis=1)
        pieces = jnp.where(row == 0, first, jnp.where(row == 1, second, 0.0))
        buf[h, 4 * TOK :, :] = pieces.astype(BF16)
    stores = []
    for h in range(HEADS):
        for copy in copies[h]:
            copy.wait()
        stores.append(pltpu.make_async_copy(buf.at[h], out_ref.at[h], out_sems.at[h]))
        stores[-1].start()
    for store in stores:
        store.wait()


def part(ref, c, n):
    per = CHUNK // TOK
    return ref[c * per : (c + 1) * per, n * TOK : (n + 1) * TOK, :].reshape(CHUNK, 256)


def put(ref, c, n, item):
    per = CHUNK // TOK
    item = item.astype(BF16).reshape(per, TOK, 256)
    ref[c * per : (c + 1) * per, n * TOK : (n + 1) * TOK, :] = item


def rows_of(ref, c, n):
    per = CHUNK // TOK
    return ref.at[c * per : (c + 1) * per, n * TOK : (n + 1) * TOK, :]


def send(source, target, sems, c, n):
    copy = pltpu.make_async_copy(rows_of(source, c, n), rows_of(target, c, n), sems.at[n, c])
    copy.start()
    return copy


def chunk_decay(col_ref, row_ref, c):
    column = col_ref[:, c : c + 1]
    line = row_ref[c : c + 1, :]
    return column, line, line[:, CHUNK - 1 :]


def chunk_weight(column, line):
    t = lax.broadcasted_iota(jnp.int32, (CHUNK, CHUNK), 0)
    s = lax.broadcasted_iota(jnp.int32, (CHUNK, CHUNK), 1)
    return jnp.where(t >= s, jnp.exp(jnp.minimum(column - line, 0.0)), 0.0)


def state_kernel(got_ref, total_ref, states_ref, col_ref, row_ref, decay_ref):
    decay_ref[...] = jnp.zeros_like(decay_ref)
    for i in range(GROUP):
        pieces = got_ref[i, 4 * TOK :, :].astype(F32)
        decay = pieces[0:1, :TOK] + pieces[0:1, TOK:] + pieces[1:2, :TOK]
        c, j = divmod(i * TOK, CHUNK)
        decay_ref[c : c + 1, j : j + TOK] = decay
    decay = decay_ref[...]
    t = lax.broadcasted_iota(jnp.int32, (CHUNK, CHUNK), 0)
    s = lax.broadcasted_iota(jnp.int32, (CHUNK, CHUNK), 1)
    lower = (t >= s).astype(F32)
    exact = dict(precision=lax.Precision.HIGHEST, preferred_element_type=F32)
    row_ref[...] = lax.dot_general(decay, lower, (((1,), (1,)), ((), ())), **exact)
    col_ref[...] = lax.dot_general(lower, decay, (((1,), (1,)), ((), ())), **exact)
    carried = jnp.zeros((KD, VD), F32)
    for c in range(CHUNKS):
        states_ref[c] = carried
        column, line, last = chunk_decay(col_ref, row_ref, c)
        key_tail = (part(got_ref, c, 1).astype(F32) * jnp.exp(last - column)).astype(BF16)
        carried = jnp.exp(last) * carried + tn(key_tail, part(got_ref, c, 2))
    total_ref[...] = carried.astype(BF16)


def local_kernel(got_ref, states_ref, col_ref, row_ref, retained_ref, output_ref):
    for c in range(CHUNKS):
        column, line, last = chunk_decay(col_ref, row_ref, c)
        q = part(got_ref, c, 0)
        scores = nt(q, part(got_ref, c, 1))
        retained = (scores * (SCALE * chunk_weight(column, line))).astype(BF16)
        retained_ref[c] = retained
        output = nn(retained, part(got_ref, c, 2))
        if c:
            tail = (q.astype(F32) * (SCALE * jnp.exp(column))).astype(BF16)
            output = output + nn(tail, states_ref[c].astype(BF16))
        output_ref[c] = output


def output_kernel(
    where_ref, got_ref, states_ref, retained_ref, output_ref, middle_ref, col_ref, row_ref, gain_ref,
    out_ref, total_ref, gain_part_ref, back_ref, total_buf, block_grads, keys_acc, values_acc, sems,
):
    copies = []
    gain = gain_ref[0:1, :]
    middle = jnp.where(where_ref[0] > 0, middle_ref[...].astype(F32), 0.0)
    middle_low = middle.astype(BF16)
    before = jnp.zeros((1, 1), F32)
    gain_part = jnp.zeros((1, VD), F32)
    for c in range(CHUNKS):
        column, line, last = chunk_decay(col_ref, row_ref, c)
        q, k, v = part(got_ref, c, 0), part(got_ref, c, 1), part(got_ref, c, 2)
        from_start = SCALE * jnp.exp(column)
        tail = (q.astype(F32) * from_start).astype(BF16)
        state_in = (states_ref[c] + jnp.exp(before) * middle).astype(BF16)
        output = output_ref[c] + jnp.exp(before) * nn(tail, middle_low)
        before = before + last
        centred = output - jnp.mean(output, axis=1, keepdims=True)
        inverse = lax.rsqrt(jnp.mean(centred * centred, axis=1, keepdims=True) + EPSILON)
        normed = centred * inverse
        wide = part(got_ref, c, 3).astype(F32)
        gain_part = gain_part + jnp.sum(wide * normed, axis=0, keepdims=True)
        scaled = wide * gain
        grad = inverse * (
            scaled
            - jnp.mean(scaled, axis=1, keepdims=True)
            - normed * jnp.mean(scaled * normed, axis=1, keepdims=True)
        )
        grad = grad.astype(BF16)
        block_grads[c] = tn(tail, grad)
        scores = nt(grad, v)
        grad_retained = (scores * (SCALE * chunk_weight(column, line))).astype(BF16)
        queries = nn(grad_retained, k) + from_start * nt(grad, state_in)
        put(back_ref, c, 0, queries)
        copies.append(send(back_ref, out_ref, sems, c, 0))
        keys_acc[c] = tn(grad_retained, q)
        values_acc[c] = tn(retained_ref[c], grad)
    carried = jnp.zeros((KD, VD), F32)
    for c in reversed(range(CHUNKS)):
        column, _, last = chunk_decay(col_ref, row_ref, c)
        keys, values = keys_acc[c], values_acc[c]
        if c < CHUNKS - 1:
            to_end = jnp.exp(last - column)
            after = carried.astype(BF16)
            keys = keys + to_end * nt(part(got_ref, c, 2), after)
            values = values + to_end * nn(part(got_ref, c, 1), after)
        put(back_ref, c, 1, keys)
        put(back_ref, c, 2, values)
        copies.append(send(back_ref, out_ref, sems, c, 1))
        copies.append(send(back_ref, out_ref, sems, c, 2))
        carried = jnp.exp(last) * carried + block_grads[c]
    total_buf[...] = carried.astype(BF16)
    copies.append(pltpu.make_async_copy(total_buf, total_ref, sems.at[3, 0]))
    copies[-1].start()
    mine = lax.broadcasted_iota(jnp.int32, (HEADS, VD), 0) == where_ref[1]
    gain_part_ref[...] = jnp.where(mine, gain_part, 0.0)
    for copy in copies:
        copy.wait()


def spread_kernel(gain_ref, out_ref):
    for i in range(out_ref.shape[0]):
        out_ref[i] = gain_ref[...]


def last_kernel(where_ref, got_ref, back_ref, middle_ref, col_ref, row_ref, out_ref, buf, sems, out_sems):
    fetches = {}
    for c in reversed(range(CHUNKS)):
        for n in (1, 2):
            fetches[c, n] = send(back_ref, buf, sems, c, n)
    middle = jnp.where(where_ref[0] > 0, 0.0, middle_ref[...].astype(F32)).astype(BF16)
    after = jnp.zeros((1, 1), F32)
    copies = []
    for c in reversed(range(CHUNKS)):
        column, line, last = chunk_decay(col_ref, row_ref, c)
        to_end = jnp.exp(after + (last - column))
        after = after + last
        keys = to_end * nt(part(got_ref, c, 2), middle)
        values = to_end * nn(part(got_ref, c, 1), middle)
        for n, item in ((1, keys), (2, values)):
            fetches[c, n].wait()
            put(buf, c, n, part(buf, c, n).astype(F32) + item)
            copies.append(send(buf, out_ref, out_sems, c, n))
    for copy in copies:
        copy.wait()


def unpack_kernel(got_ref, queries_ref, keys_ref, values_ref, sems):
    copies = []
    for n, ref in enumerate((queries_ref, keys_ref, values_ref)):
        for h in range(HEADS):
            copies.append(
                pltpu.make_async_copy(
                    got_ref.at[h, n * TOK : (n + 1) * TOK, :],
                    ref.at[:, h * KD : (h + 1) * KD],
                    sems.at[n * HEADS + h],
                )
            )
    for copy in copies:
        copy.start()
    for copy in copies:
        copy.wait()


def shards(queries, key_vectors, values, grad_out, log_decay, norm_gain):
    place = lax.axis_index("ctx")
    blocks = lax.axis_size("ctx")
    halves = [list(range(GROUP)), list(range(GROUP, 2 * GROUP))]
    size = lax.axis_size("dp")
    swap = [(i, i ^ GROUP) for i in range(blocks)]
    where = jnp.stack([place // GROUP, place % GROUP]).astype(jnp.int32)
    gain = lax.dynamic_slice_in_dim(norm_gain.reshape(HEADS, VD), place % GROUP, 1, 0)
    square = (CHUNKS, CHUNK, 256)

    packed = call(
        pack_kernel,
        [((GROUP, ROWS, 256), BF16)],
        [
            pltpu.VMEM((GROUP, ROWS, 256), BF16),
            pltpu.VMEM((HEADS, TOK), F32),
            pltpu.SemaphoreType.DMA((HEADS, 4)),
            pltpu.SemaphoreType.DMA,
            pltpu.SemaphoreType.DMA((HEADS,)),
        ],
        places={i: pltpu.HBM for i in range(5)},
        far=(0,),
    )(queries[0], key_vectors[0], values[0], grad_out[0], log_decay[0])[0]
    got = lax.all_to_all(packed, "ctx", 0, 0, axis_index_groups=halves, tiled=True)
    total, states, column, line = call(
        state_kernel,
        [((KD, VD), BF16), ((CHUNKS, KD, VD), F32), ((CHUNK, 8), F32), ((8, CHUNK), F32)],
        [pltpu.VMEM((8, CHUNK), F32)],
    )(got)
    middle = lax.ppermute(total, "ctx", swap)
    retained, output = call(local_kernel, [(square, BF16), (square, F32)])(
        got, states, column, line
    )
    back, total_grad, gain_part = call(
        output_kernel,
        [((GROUP, BACK, 256), BF16), ((KD, VD), BF16), ((HEADS, VD), F32)],
        [
            pltpu.VMEM((GROUP, BACK, 256), BF16),
            pltpu.VMEM((KD, VD), BF16),
            *[pltpu.VMEM((CHUNKS, 256, 256), F32)] * 3,
            pltpu.SemaphoreType.DMA((4, CHUNKS)),
        ],
        places={0: pltpu.SMEM},
        far=(0, 1),
    )(where, got, states, retained, output, middle, column, line, gain)
    middle_grad = lax.ppermute(total_grad, "ctx", swap)
    gains = lax.all_to_all(
        call(spread_kernel, [((blocks, HEADS, VD), F32)], cost=(4 * 10**9, 2**20))(gain_part)[0],
        "ctx", 0, 0, tiled=True,
    )
    back = call(
        last_kernel,
        [((GROUP, BACK, 256), BF16)],
        [pltpu.VMEM((GROUP, BACK, 256), BF16), *[pltpu.SemaphoreType.DMA((3, CHUNKS))] * 2],
        places={0: pltpu.SMEM, 2: pltpu.HBM},
        far=(0,),
        aliases={2: 0},
    )(where, got, back, middle_grad, column, line)[0]
    back = lax.all_to_all(back, "ctx", 0, 0, axis_index_groups=halves, tiled=True)
    gain_rows = jnp.pad(jnp.sum(gains, axis=0), ((0, 24), (0, 0)))
    gain_all = lax.all_gather(gain_rows, "dp")[:, :HEADS]
    results = call(
        unpack_kernel,
        [((TOK, HEADS * KD), BF16)] * 3,
        [pltpu.SemaphoreType.DMA((3 * HEADS,))],
        places={0: pl.ANY},
        far=(0, 1, 2),
    )(back)
    grad_gain = (jnp.sum(gain_all, axis=0) / size).reshape(HEADS * VD)
    return (*(item[None] for item in results), grad_gain)


def solution(mesh):
    return jax.shard_map(
        shards,
        mesh=mesh,
        in_specs=(
            P("dp", "ctx", None),
            P("dp", "ctx", None),
            P("dp", "ctx", None),
            P("dp", "ctx", None),
            P("dp", None, "ctx"),
            P(),
        ),
        out_specs=(P("dp", "ctx", None), P("dp", "ctx", None), P("dp", "ctx", None), P()),
        check_vma=False,
    )
```

```python
import jax
import jax.numpy as jnp
from jax import lax
from jax.experimental import pallas as pl
from jax.experimental.pallas import tpu as pltpu
from jax.sharding import PartitionSpec as P

HEADS = 8
KD = 256
VD = 256
EPSILON = 1e-05

TOK = 128
GROUP = 8
CHUNK = 256
CHUNKS = GROUP * TOK // CHUNK
ROWS = 4 * TOK + 16
BACK = 3 * TOK

F32 = jnp.float32
BF16 = jnp.bfloat16
SCALE = KD ** (-0.5)


def nn(a, b):
    return lax.dot_general(a, b, (((1,), (0,)), ((), ())), preferred_element_type=F32)


def nt(a, b):
    return lax.dot_general(a, b, (((1,), (1,)), ((), ())), preferred_element_type=F32)


def tn(a, b):
    return lax.dot_general(a, b, (((0,), (0,)), ((), ())), preferred_element_type=F32)


def call(kernel, outs, scratch=(), places=None, far=(), cost=None, aliases=None):
    def run(*args):
        where = places or {}
        args = [
            pltpu.with_memory_space_constraint(item, pltpu.HBM) if where.get(i) == pltpu.HBM else item
            for i, item in enumerate(args)
        ]
        return pl.pallas_call(
            kernel,
            out_shape=[
                (pltpu.HBM if i in far else jax.ShapeDtypeStruct)(shape, kind)
                for i, (shape, kind) in enumerate(outs)
            ],
            in_specs=[
                pl.BlockSpec(memory_space=where.get(i, pltpu.VMEM)) for i in range(len(args))
            ],
            out_specs=[
                pl.BlockSpec(memory_space=pltpu.HBM if i in far else pltpu.VMEM)
                for i in range(len(outs))
            ],
            scratch_shapes=list(scratch),
            compiler_params=pltpu.CompilerParams(vmem_limit_bytes=16 * 1024 * 1024),
            cost_estimate=cost and pl.CostEstimate(flops=cost[0], bytes_accessed=cost[1], transcendentals=0),
            input_output_aliases=aliases or {},
        )(*args)

    return run


def pack_kernel(
    q_ref, k_ref, v_ref, g_ref, decay_ref, out_ref, buf, decay_buf, sems, decay_sem, out_sems
):
    fetch = pltpu.make_async_copy(decay_ref, decay_buf, decay_sem)
    fetch.start()
    copies = [
        [
            pltpu.make_async_copy(
                ref.at[:, h * KD : (h + 1) * KD],
                buf.at[h, n * TOK : (n + 1) * TOK, :],
                sems.at[h, n],
            )
            for n, ref in enumerate((q_ref, k_ref, v_ref, g_ref))
        ]
        for h in range(HEADS)
    ]
    for copy in sum(copies, []):
        copy.start()
    fetch.wait()
    row = lax.broadcasted_iota(jnp.int32, (16, 256), 0)
    for h in range(HEADS):
        decay = decay_buf[h : h + 1, :]
        high = decay.astype(BF16).astype(F32)
        rest = decay - high
        middle = rest.astype(BF16).astype(F32)
        low = rest - middle
        first = jnp.concatenate([high, middle], axis=1)
        second = jnp.concatenate([low, jnp.zeros_like(low)], axis=1)
        pieces = jnp.where(row == 0, first, jnp.where(row == 1, second, 0.0))
        buf[h, 4 * TOK :, :] = pieces.astype(BF16)
    stores = []
    for h in range(HEADS):
        for copy in copies[h]:
            copy.wait()
        stores.append(pltpu.make_async_copy(buf.at[h], out_ref.at[h], out_sems.at[h]))
        stores[-1].start()
    for store in stores:
        store.wait()


def part(ref, c, n):
    per = CHUNK // TOK
    return ref[c * per : (c + 1) * per, n * TOK : (n + 1) * TOK, :].reshape(CHUNK, 256)


def put(ref, c, n, item):
    per = CHUNK // TOK
    item = item.astype(BF16).reshape(per, TOK, 256)
    ref[c * per : (c + 1) * per, n * TOK : (n + 1) * TOK, :] = item


def rows_of(ref, c, n):
    per = CHUNK // TOK
    return ref.at[c * per : (c + 1) * per, n * TOK : (n + 1) * TOK, :]


def send(source, target, sems, c, n):
    copy = pltpu.make_async_copy(rows_of(source, c, n), rows_of(target, c, n), sems.at[n, c])
    copy.start()
    return copy


def chunk_decay(col_ref, row_ref, c):
    column = col_ref[:, c : c + 1]
    line = row_ref[c : c + 1, :]
    return column, line, line[:, CHUNK - 1 :]


def chunk_weight(column, line):
    t = lax.broadcasted_iota(jnp.int32, (CHUNK, CHUNK), 0)
    s = lax.broadcasted_iota(jnp.int32, (CHUNK, CHUNK), 1)
    return jnp.where(t >= s, jnp.exp(jnp.minimum(column - line, 0.0)), 0.0)


def state_kernel(got_ref, total_ref, states_ref, col_ref, row_ref, decay_ref):
    decay_ref[...] = jnp.zeros_like(decay_ref)
    for i in range(GROUP):
        pieces = got_ref[i, 4 * TOK :, :].astype(F32)
        decay = pieces[0:1, :TOK] + pieces[0:1, TOK:] + pieces[1:2, :TOK]
        c, j = divmod(i * TOK, CHUNK)
        decay_ref[c : c + 1, j : j + TOK] = decay
    decay = decay_ref[...]
    t = lax.broadcasted_iota(jnp.int32, (CHUNK, CHUNK), 0)
    s = lax.broadcasted_iota(jnp.int32, (CHUNK, CHUNK), 1)
    lower = (t >= s).astype(F32)
    exact = dict(precision=lax.Precision.HIGHEST, preferred_element_type=F32)
    row_ref[...] = lax.dot_general(decay, lower, (((1,), (1,)), ((), ())), **exact)
    col_ref[...] = lax.dot_general(lower, decay, (((1,), (1,)), ((), ())), **exact)
    carried = jnp.zeros((KD, VD), F32)
    for c in range(CHUNKS):
        states_ref[c] = carried
        column, line, last = chunk_decay(col_ref, row_ref, c)
        key_tail = (part(got_ref, c, 1).astype(F32) * jnp.exp(last - column)).astype(BF16)
        carried = jnp.exp(last) * carried + tn(key_tail, part(got_ref, c, 2))
    total_ref[...] = carried.astype(BF16)


def local_kernel(got_ref, states_ref, col_ref, row_ref, retained_ref, output_ref):
    for c in range(CHUNKS):
        column, line, last = chunk_decay(col_ref, row_ref, c)
        q = part(got_ref, c, 0)
        scores = nt(q, part(got_ref, c, 1))
        retained = (scores * (SCALE * chunk_weight(column, line))).astype(BF16)
        retained_ref[c] = retained
        output = nn(retained, part(got_ref, c, 2))
        if c:
            tail = (q.astype(F32) * (SCALE * jnp.exp(column))).astype(BF16)
            output = output + nn(tail, states_ref[c].astype(BF16))
        output_ref[c] = output


def output_kernel(
    where_ref, got_ref, states_ref, retained_ref, output_ref, middle_ref, col_ref, row_ref, gain_ref,
    out_ref, total_ref, gain_part_ref, back_ref, total_buf, block_grads, keys_acc, values_acc, sems,
):
    copies = []
    gain = gain_ref[0:1, :]
    middle = jnp.where(where_ref[0] > 0, middle_ref[...].astype(F32), 0.0)
    middle_low = middle.astype(BF16)
    before = jnp.zeros((1, 1), F32)
    gain_part = jnp.zeros((1, VD), F32)
    for c in range(CHUNKS):
        column, line, last = chunk_decay(col_ref, row_ref, c)
        q, k, v = part(got_ref, c, 0), part(got_ref, c, 1), part(got_ref, c, 2)
        from_start = SCALE * jnp.exp(column)
        tail = (q.astype(F32) * from_start).astype(BF16)
        state_in = (states_ref[c] + jnp.exp(before) * middle).astype(BF16)
        output = output_ref[c] + jnp.exp(before) * nn(tail, middle_low)
        before = before + last
        centred = output - jnp.mean(output, axis=1, keepdims=True)
        inverse = lax.rsqrt(jnp.mean(centred * centred, axis=1, keepdims=True) + EPSILON)
        normed = centred * inverse
        wide = part(got_ref, c, 3).astype(F32)
        gain_part = gain_part + jnp.sum(wide * normed, axis=0, keepdims=True)
        scaled = wide * gain
        grad = inverse * (
            scaled
            - jnp.mean(scaled, axis=1, keepdims=True)
            - normed * jnp.mean(scaled * normed, axis=1, keepdims=True)
        )
        grad = grad.astype(BF16)
        block_grads[c] = tn(tail, grad)
        scores = nt(grad, v)
        grad_retained = (scores * (SCALE * chunk_weight(column, line))).astype(BF16)
        queries = nn(grad_retained, k) + from_start * nt(grad, state_in)
        put(back_ref, c, 0, queries)
        copies.append(send(back_ref, out_ref, sems, c, 0))
        keys_acc[c] = tn(grad_retained, q)
        values_acc[c] = tn(retained_ref[c], grad)
    carried = jnp.zeros((KD, VD), F32)
    for c in reversed(range(CHUNKS)):
        column, _, last = chunk_decay(col_ref, row_ref, c)
        keys, values = keys_acc[c], values_acc[c]
        if c < CHUNKS - 1:
            to_end = jnp.exp(last - column)
            after = carried.astype(BF16)
            keys = keys + to_end * nt(part(got_ref, c, 2), after)
            values = values + to_end * nn(part(got_ref, c, 1), after)
        put(back_ref, c, 1, keys)
        put(back_ref, c, 2, values)
        copies.append(send(back_ref, out_ref, sems, c, 1))
        copies.append(send(back_ref, out_ref, sems, c, 2))
        carried = jnp.exp(last) * carried + block_grads[c]
    total_buf[...] = carried.astype(BF16)
    copies.append(pltpu.make_async_copy(total_buf, total_ref, sems.at[3, 0]))
    copies[-1].start()
    mine = lax.broadcasted_iota(jnp.int32, (HEADS, VD), 0) == where_ref[1]
    gain_part_ref[...] = jnp.where(mine, gain_part, 0.0)
    for copy in copies:
        copy.wait()


def spread_kernel(gain_ref, out_ref):
    for i in range(out_ref.shape[0]):
        out_ref[i] = gain_ref[...]


def last_kernel(where_ref, got_ref, back_ref, middle_ref, col_ref, row_ref, out_ref, buf, sems, out_sems):
    fetches = {}
    for c in reversed(range(CHUNKS)):
        for n in (1, 2):
            fetches[c, n] = send(back_ref, buf, sems, c, n)
    middle = jnp.where(where_ref[0] > 0, 0.0, middle_ref[...].astype(F32)).astype(BF16)
    after = jnp.zeros((1, 1), F32)
    copies = []
    for c in reversed(range(CHUNKS)):
        column, line, last = chunk_decay(col_ref, row_ref, c)
        to_end = jnp.exp(after + (last - column))
        after = after + last
        keys = to_end * nt(part(got_ref, c, 2), middle)
        values = to_end * nn(part(got_ref, c, 1), middle)
        for n, item in ((1, keys), (2, values)):
            fetches[c, n].wait()
            put(buf, c, n, part(buf, c, n).astype(F32) + item)
            copies.append(send(buf, out_ref, out_sems, c, n))
    for copy in copies:
        copy.wait()


def unpack_kernel(got_ref, queries_ref, keys_ref, values_ref, sems):
    copies = []
    for n, ref in enumerate((queries_ref, keys_ref, values_ref)):
        for h in range(HEADS):
            copies.append(
                pltpu.make_async_copy(
                    got_ref.at[h, n * TOK : (n + 1) * TOK, :],
                    ref.at[:, h * KD : (h + 1) * KD],
                    sems.at[n * HEADS + h],
                )
            )
    for copy in copies:
        copy.start()
    for copy in copies:
        copy.wait()


def shards(queries, key_vectors, values, grad_out, log_decay, norm_gain):
    place = lax.axis_index("ctx")
    blocks = lax.axis_size("ctx")
    halves = [list(range(GROUP)), list(range(GROUP, 2 * GROUP))]
    size = lax.axis_size("dp")
    swap = [(i, i ^ GROUP) for i in range(blocks)]
    where = jnp.stack([place // GROUP, place % GROUP]).astype(jnp.int32)
    gain = lax.dynamic_slice_in_dim(norm_gain.reshape(HEADS, VD), place % GROUP, 1, 0)
    square = (CHUNKS, CHUNK, 256)

    packed = call(
        pack_kernel,
        [((GROUP, ROWS, 256), BF16)],
        [
            pltpu.VMEM((GROUP, ROWS, 256), BF16),
            pltpu.VMEM((HEADS, TOK), F32),
            pltpu.SemaphoreType.DMA((HEADS, 4)),
            pltpu.SemaphoreType.DMA,
            pltpu.SemaphoreType.DMA((HEADS,)),
        ],
        places={i: pltpu.HBM for i in range(5)},
        far=(0,),
    )(queries[0], key_vectors[0], values[0], grad_out[0], log_decay[0])[0]
    got = lax.all_to_all(packed, "ctx", 0, 0, axis_index_groups=halves, tiled=True)
    total, states, column, line = call(
        state_kernel,
        [((KD, VD), BF16), ((CHUNKS, KD, VD), F32), ((CHUNK, 8), F32), ((8, CHUNK), F32)],
        [pltpu.VMEM((8, CHUNK), F32)],
    )(got)
    middle = lax.ppermute(total, "ctx", swap)
    retained, output = call(local_kernel, [(square, BF16), (square, F32)])(
        got, states, column, line
    )
    back, total_grad, gain_part = call(
        output_kernel,
        [((GROUP, BACK, 256), BF16), ((KD, VD), BF16), ((HEADS, VD), F32)],
        [
            pltpu.VMEM((GROUP, BACK, 256), BF16),
            pltpu.VMEM((KD, VD), BF16),
            *[pltpu.VMEM((CHUNKS, 256, 256), F32)] * 3,
            pltpu.SemaphoreType.DMA((4, CHUNKS)),
        ],
        places={0: pltpu.SMEM},
        far=(0, 1),
    )(where, got, states, retained, output, middle, column, line, gain)
    middle_grad = lax.ppermute(total_grad, "ctx", swap)
    gains = lax.all_to_all(
        call(spread_kernel, [((blocks, HEADS, VD), F32)], cost=(4 * 10**9, 2**20))(gain_part)[0],
        "ctx", 0, 0, tiled=True,
    )
    back = call(
        last_kernel,
        [((GROUP, BACK, 256), BF16)],
        [pltpu.VMEM((GROUP, BACK, 256), BF16), *[pltpu.SemaphoreType.DMA((3, CHUNKS))] * 2],
        places={0: pltpu.SMEM, 2: pltpu.HBM},
        far=(0,),
        aliases={2: 0},
    )(where, got, back, middle_grad, column, line)[0]
    back = lax.all_to_all(back, "ctx", 0, 0, axis_index_groups=halves, tiled=True)
    gain_sum = jnp.sum(gains, axis=0)
    near = [list(range(i, i + 8)) for i in range(0, size, 8)]
    apart = [list(range(i, size, 8)) for i in range(8)]
    for groups in (near, apart):
        gain_sum = jnp.sum(lax.all_gather(gain_sum, "dp", axis_index_groups=groups), axis=0)
    results = call(
        unpack_kernel,
        [((TOK, HEADS * KD), BF16)] * 3,
        [pltpu.SemaphoreType.DMA((3 * HEADS,))],
        places={0: pl.ANY},
        far=(0, 1, 2),
    )(back)
    grad_gain = (gain_sum / size).reshape(HEADS * VD)
    return (*(item[None] for item in results), grad_gain)


def solution(mesh):
    return jax.shard_map(
        shards,
        mesh=mesh,
        in_specs=(
            P("dp", "ctx", None),
            P("dp", "ctx", None),
            P("dp", "ctx", None),
            P("dp", "ctx", None),
            P("dp", None, "ctx"),
            P(),
        ),
        out_specs=(P("dp", "ctx", None), P("dp", "ctx", None), P("dp", "ctx", None), P()),
        check_vma=False,
    )
```

```python
import jax
import jax.numpy as jnp
from jax import lax
from jax.experimental import pallas as pl
from jax.experimental.pallas import tpu as pltpu
from jax.sharding import PartitionSpec as P

HEADS = 8
KD = 256
VD = 256
EPSILON = 1e-05

TOK = 128
GROUP = 8
CHUNK = 256
CHUNKS = GROUP * TOK // CHUNK
ROWS = 4 * TOK + 16
BACK = 3 * TOK

F32 = jnp.float32
BF16 = jnp.bfloat16
SCALE = KD ** (-0.5)


def nn(a, b):
    return lax.dot_general(a, b, (((1,), (0,)), ((), ())), preferred_element_type=F32)


def nt(a, b):
    return lax.dot_general(a, b, (((1,), (1,)), ((), ())), preferred_element_type=F32)


def tn(a, b):
    return lax.dot_general(a, b, (((0,), (0,)), ((), ())), preferred_element_type=F32)


def call(kernel, outs, scratch=(), places=None, far=(), cost=None, aliases=None):
    def run(*args):
        where = places or {}
        args = [
            pltpu.with_memory_space_constraint(item, pltpu.HBM) if where.get(i) == pltpu.HBM else item
            for i, item in enumerate(args)
        ]
        return pl.pallas_call(
            kernel,
            out_shape=[
                (pltpu.HBM if i in far else jax.ShapeDtypeStruct)(shape, kind)
                for i, (shape, kind) in enumerate(outs)
            ],
            in_specs=[
                pl.BlockSpec(memory_space=where.get(i, pltpu.VMEM)) for i in range(len(args))
            ],
            out_specs=[
                pl.BlockSpec(memory_space=pltpu.HBM if i in far else pltpu.VMEM)
                for i in range(len(outs))
            ],
            scratch_shapes=list(scratch),
            compiler_params=pltpu.CompilerParams(vmem_limit_bytes=16 * 1024 * 1024),
            cost_estimate=cost and pl.CostEstimate(flops=cost[0], bytes_accessed=cost[1], transcendentals=0),
            input_output_aliases=aliases or {},
        )(*args)

    return run


def pack_kernel(
    q_ref, k_ref, v_ref, g_ref, decay_ref, out_ref, buf, decay_buf, sems, decay_sem, out_sems
):
    fetch = pltpu.make_async_copy(decay_ref, decay_buf, decay_sem)
    fetch.start()
    copies = [
        [
            pltpu.make_async_copy(
                ref.at[:, h * KD : (h + 1) * KD],
                buf.at[h, n * TOK : (n + 1) * TOK, :],
                sems.at[h, n],
            )
            for n, ref in enumerate((q_ref, k_ref, v_ref, g_ref))
        ]
        for h in range(HEADS)
    ]
    for copy in sum(copies, []):
        copy.start()
    fetch.wait()
    row = lax.broadcasted_iota(jnp.int32, (16, 256), 0)
    for h in range(HEADS):
        decay = decay_buf[h : h + 1, :]
        high = decay.astype(BF16).astype(F32)
        rest = decay - high
        middle = rest.astype(BF16).astype(F32)
        low = rest - middle
        first = jnp.concatenate([high, middle], axis=1)
        second = jnp.concatenate([low, jnp.zeros_like(low)], axis=1)
        pieces = jnp.where(row == 0, first, jnp.where(row == 1, second, 0.0))
        buf[h, 4 * TOK :, :] = pieces.astype(BF16)
    stores = []
    for h in range(HEADS):
        for copy in copies[h]:
            copy.wait()
        stores.append(pltpu.make_async_copy(buf.at[h], out_ref.at[h], out_sems.at[h]))
        stores[-1].start()
    for store in stores:
        store.wait()


def part(ref, c, n):
    per = CHUNK // TOK
    return ref[c * per : (c + 1) * per, n * TOK : (n + 1) * TOK, :].reshape(CHUNK, 256)


def put(ref, c, n, item):
    per = CHUNK // TOK
    item = item.astype(BF16).reshape(per, TOK, 256)
    ref[c * per : (c + 1) * per, n * TOK : (n + 1) * TOK, :] = item


def rows_of(ref, c, n):
    per = CHUNK // TOK
    return ref.at[c * per : (c + 1) * per, n * TOK : (n + 1) * TOK, :]


def send(source, target, sems, c, n):
    copy = pltpu.make_async_copy(rows_of(source, c, n), rows_of(target, c, n), sems.at[n, c])
    copy.start()
    return copy


def chunk_decay(col_ref, row_ref, c):
    column = col_ref[:, c : c + 1]
    line = row_ref[c : c + 1, :]
    return column, line, line[:, CHUNK - 1 :]


def chunk_weight(column, line):
    t = lax.broadcasted_iota(jnp.int32, (CHUNK, CHUNK), 0)
    s = lax.broadcasted_iota(jnp.int32, (CHUNK, CHUNK), 1)
    return jnp.where(t >= s, jnp.exp(jnp.minimum(column - line, 0.0)), 0.0)


def state_kernel(got_ref, total_ref, states_ref, col_ref, row_ref, decay_ref):
    decay_ref[...] = jnp.zeros_like(decay_ref)
    for i in range(GROUP):
        pieces = got_ref[i, 4 * TOK :, :].astype(F32)
        c, j = divmod(i * TOK, CHUNK)
        for n, piece in enumerate((pieces[0:1, :TOK], pieces[0:1, TOK:], pieces[1:2, :TOK])):
            decay_ref[8 * n + c : 8 * n + c + 1, j : j + TOK] = piece
    pieces = decay_ref[...].astype(BF16)
    t = lax.broadcasted_iota(jnp.int32, (CHUNK, CHUNK), 0)
    s = lax.broadcasted_iota(jnp.int32, (CHUNK, CHUNK), 1)
    lower = (t >= s).astype(F32).astype(BF16)
    lines = nt(pieces, lower)
    row_ref[...] = (lines[0:8] + lines[8:16]) + lines[16:24]
    columns = nt(lower, pieces)
    col_ref[...] = (columns[:, 0:8] + columns[:, 8:16]) + columns[:, 16:24]
    carried = jnp.zeros((KD, VD), F32)
    for c in range(CHUNKS):
        states_ref[c] = carried
        column, line, last = chunk_decay(col_ref, row_ref, c)
        key_tail = (part(got_ref, c, 1).astype(F32) * jnp.exp(last - column)).astype(BF16)
        carried = jnp.exp(last) * carried + tn(key_tail, part(got_ref, c, 2))
    total_ref[...] = carried.astype(BF16)


def local_kernel(got_ref, states_ref, col_ref, row_ref, retained_ref, output_ref):
    for c in range(CHUNKS):
        column, line, last = chunk_decay(col_ref, row_ref, c)
        q = part(got_ref, c, 0)
        scores = nt(q, part(got_ref, c, 1))
        retained = (scores * (SCALE * chunk_weight(column, line))).astype(BF16)
        retained_ref[c] = retained
        output = nn(retained, part(got_ref, c, 2))
        if c:
            tail = (q.astype(F32) * (SCALE * jnp.exp(column))).astype(BF16)
            output = output + nn(tail, states_ref[c].astype(BF16))
        output_ref[c] = output


def output_kernel(
    where_ref, got_ref, states_ref, retained_ref, output_ref, middle_ref, col_ref, row_ref, gain_ref,
    out_ref, total_ref, gain_part_ref, back_ref, total_buf, block_grads, keys_acc, values_acc, sems,
):
    copies = []
    gain = gain_ref[0:1, :]
    middle = jnp.where(where_ref[0] > 0, middle_ref[...].astype(F32), 0.0)
    middle_low = middle.astype(BF16)
    before = jnp.zeros((1, 1), F32)
    gain_part = jnp.zeros((1, VD), F32)
    for c in range(CHUNKS):
        column, line, last = chunk_decay(col_ref, row_ref, c)
        q, k, v = part(got_ref, c, 0), part(got_ref, c, 1), part(got_ref, c, 2)
        from_start = SCALE * jnp.exp(column)
        tail = (q.astype(F32) * from_start).astype(BF16)
        state_in = (states_ref[c] + jnp.exp(before) * middle).astype(BF16)
        output = output_ref[c] + jnp.exp(before) * nn(tail, middle_low)
        before = before + last
        centred = output - jnp.mean(output, axis=1, keepdims=True)
        inverse = lax.rsqrt(jnp.mean(centred * centred, axis=1, keepdims=True) + EPSILON)
        normed = centred * inverse
        wide = part(got_ref, c, 3).astype(F32)
        gain_part = gain_part + jnp.sum(wide * normed, axis=0, keepdims=True)
        scaled = wide * gain
        grad = inverse * (
            scaled
            - jnp.mean(scaled, axis=1, keepdims=True)
            - normed * jnp.mean(scaled * normed, axis=1, keepdims=True)
        )
        grad = grad.astype(BF16)
        block_grads[c] = tn(tail, grad)
        scores = nt(grad, v)
        grad_retained = (scores * (SCALE * chunk_weight(column, line))).astype(BF16)
        queries = nn(grad_retained, k) + from_start * nt(grad, state_in)
        put(back_ref, c, 0, queries)
        copies.append(send(back_ref, out_ref, sems, c, 0))
        keys_acc[c] = tn(grad_retained, q)
        values_acc[c] = tn(retained_ref[c], grad)
    carried = jnp.zeros((KD, VD), F32)
    for c in reversed(range(CHUNKS)):
        column, _, last = chunk_decay(col_ref, row_ref, c)
        keys, values = keys_acc[c], values_acc[c]
        if c < CHUNKS - 1:
            to_end = jnp.exp(last - column)
            after = carried.astype(BF16)
            keys = keys + to_end * nt(part(got_ref, c, 2), after)
            values = values + to_end * nn(part(got_ref, c, 1), after)
        put(back_ref, c, 1, keys)
        put(back_ref, c, 2, values)
        copies.append(send(back_ref, out_ref, sems, c, 1))
        copies.append(send(back_ref, out_ref, sems, c, 2))
        carried = jnp.exp(last) * carried + block_grads[c]
    total_buf[...] = carried.astype(BF16)
    copies.append(pltpu.make_async_copy(total_buf, total_ref, sems.at[3, 0]))
    copies[-1].start()
    gain_part_ref[...] = jnp.zeros_like(gain_part_ref)
    gain_part_ref[0:1, :] = gain_part[:, :128]
    gain_part_ref[1:2, :] = gain_part[:, 128:]
    for copy in copies:
        copy.wait()


def spread_kernel(gain_ref, out_ref):
    for i in range(out_ref.shape[0]):
        out_ref[i] = gain_ref[...]


def fold_kernel(gains_ref, out_ref):
    for h in range(HEADS):
        for j in range(2):
            both = gains_ref[h, j : j + 1, :] + gains_ref[h + GROUP, j : j + 1, :]
            out_ref[2 * h + j : 2 * h + j + 1, :] = both


def last_kernel(where_ref, got_ref, back_ref, middle_ref, col_ref, row_ref, out_ref, buf, sems, out_sems):
    fetches = {}
    for c in reversed(range(CHUNKS)):
        for n in (1, 2):
            fetches[c, n] = send(back_ref, buf, sems, c, n)
    middle = jnp.where(where_ref[0] > 0, 0.0, middle_ref[...].astype(F32)).astype(BF16)
    after = jnp.zeros((1, 1), F32)
    copies = []
    for c in reversed(range(CHUNKS)):
        column, line, last = chunk_decay(col_ref, row_ref, c)
        to_end = jnp.exp(after + (last - column))
        after = after + last
        keys = to_end * nt(part(got_ref, c, 2), middle)
        values = to_end * nn(part(got_ref, c, 1), middle)
        for n, item in ((1, keys), (2, values)):
            fetches[c, n].wait()
            put(buf, c, n, part(buf, c, n).astype(F32) + item)
            copies.append(send(buf, out_ref, out_sems, c, n))
    for copy in copies:
        copy.wait()


def unpack_kernel(got_ref, queries_ref, keys_ref, values_ref, sems):
    copies = []
    for n, ref in enumerate((queries_ref, keys_ref, values_ref)):
        for h in range(HEADS):
            copies.append(
                pltpu.make_async_copy(
                    got_ref.at[h, n * TOK : (n + 1) * TOK, :],
                    ref.at[:, h * KD : (h + 1) * KD],
                    sems.at[n * HEADS + h],
                )
            )
    for copy in copies:
        copy.start()
    for copy in copies:
        copy.wait()


def shards(queries, key_vectors, values, grad_out, log_decay, norm_gain):
    place = lax.axis_index("ctx")
    blocks = lax.axis_size("ctx")
    halves = [list(range(GROUP)), list(range(GROUP, 2 * GROUP))]
    size = lax.axis_size("dp")
    swap = [(i, i ^ GROUP) for i in range(blocks)]
    square = (CHUNKS, CHUNK, 256)

    packed = call(
        pack_kernel,
        [((GROUP, ROWS, 256), BF16)],
        [
            pltpu.VMEM((GROUP, ROWS, 256), BF16),
            pltpu.VMEM((HEADS, TOK), F32),
            pltpu.SemaphoreType.DMA((HEADS, 4)),
            pltpu.SemaphoreType.DMA,
            pltpu.SemaphoreType.DMA((HEADS,)),
        ],
        places={i: pltpu.HBM for i in range(5)},
        far=(0,),
    )(queries[0], key_vectors[0], values[0], grad_out[0], log_decay[0])[0]
    got = lax.all_to_all(packed, "ctx", 0, 0, axis_index_groups=halves, tiled=True)
    where = (place // GROUP).astype(jnp.int32).reshape(1)
    gain = lax.dynamic_slice_in_dim(norm_gain.reshape(HEADS, VD), place % GROUP, 1, 0)
    total, states, column, line = call(
        state_kernel,
        [((KD, VD), BF16), ((CHUNKS, KD, VD), F32), ((CHUNK, 8), F32), ((8, CHUNK), F32)],
        [pltpu.VMEM((32, CHUNK), F32)],
    )(got)
    middle = lax.ppermute(total, "ctx", swap)
    retained, output = call(local_kernel, [(square, BF16), (square, F32)])(
        got, states, column, line
    )
    back, total_grad, gain_part = call(
        output_kernel,
        [((GROUP, BACK, 256), BF16), ((KD, VD), BF16), ((8, 128), F32)],
        [
            pltpu.VMEM((GROUP, BACK, 256), BF16),
            pltpu.VMEM((KD, VD), BF16),
            *[pltpu.VMEM((CHUNKS, 256, 256), F32)] * 3,
            pltpu.SemaphoreType.DMA((4, CHUNKS)),
        ],
        places={0: pltpu.SMEM},
        far=(0, 1),
    )(where, got, states, retained, output, middle, column, line, gain)
    middle_grad = lax.ppermute(total_grad, "ctx", swap)
    gains = lax.all_to_all(
        call(spread_kernel, [((blocks, 8, 128), F32)], cost=(4 * 10**9, 2**20))(gain_part)[0],
        "ctx", 0, 0, tiled=True,
    )
    back = call(
        last_kernel,
        [((GROUP, BACK, 256), BF16)],
        [pltpu.VMEM((GROUP, BACK, 256), BF16), *[pltpu.SemaphoreType.DMA((3, CHUNKS))] * 2],
        places={0: pltpu.SMEM, 2: pltpu.HBM},
        far=(0,),
        aliases={2: 0},
    )(where, got, back, middle_grad, column, line)[0]
    back = lax.all_to_all(back, "ctx", 0, 0, axis_index_groups=halves, tiled=True)
    gain_all = lax.all_gather(call(fold_kernel, [((2 * HEADS, 128), F32)])(gains)[0], "dp")
    results = call(
        unpack_kernel,
        [((TOK, HEADS * KD), BF16)] * 3,
        [pltpu.SemaphoreType.DMA((3 * HEADS,))],
        places={0: pl.ANY},
        far=(0, 1, 2),
    )(back)
    grad_gain = (jnp.sum(gain_all, axis=0) / size).reshape(HEADS * VD)
    return (*(item[None] for item in results), grad_gain)


def solution(mesh):
    return jax.shard_map(
        shards,
        mesh=mesh,
        in_specs=(
            P("dp", "ctx", None),
            P("dp", "ctx", None),
            P("dp", "ctx", None),
            P("dp", "ctx", None),
            P("dp", None, "ctx"),
            P(),
        ),
        out_specs=(P("dp", "ctx", None), P("dp", "ctx", None), P("dp", "ctx", None), P()),
        check_vma=False,
    )
```

```python
import jax
import jax.numpy as jnp
from jax import lax
from jax.experimental import pallas as pl
from jax.experimental.pallas import tpu as pltpu
from jax.sharding import PartitionSpec as P

HEADS = 8
KD = 256
VD = 256
EPSILON = 1e-05

TOK = 128
GROUP = 8
CHUNK = 256
CHUNKS = GROUP * TOK // CHUNK
ROWS = 4 * TOK + 16
BACK = 3 * TOK

F32 = jnp.float32
BF16 = jnp.bfloat16
SCALE = KD ** (-0.5)


def nn(a, b):
    return lax.dot_general(a, b, (((1,), (0,)), ((), ())), preferred_element_type=F32)


def nt(a, b):
    return lax.dot_general(a, b, (((1,), (1,)), ((), ())), preferred_element_type=F32)


def tn(a, b):
    return lax.dot_general(a, b, (((0,), (0,)), ((), ())), preferred_element_type=F32)


def call(kernel, outs, scratch=(), places=None, far=(), cost=None, aliases=None):
    def run(*args):
        where = places or {}
        args = [
            pltpu.with_memory_space_constraint(item, pltpu.HBM) if where.get(i) == pltpu.HBM else item
            for i, item in enumerate(args)
        ]
        return pl.pallas_call(
            kernel,
            out_shape=[
                (pltpu.HBM if i in far else jax.ShapeDtypeStruct)(shape, kind)
                for i, (shape, kind) in enumerate(outs)
            ],
            in_specs=[
                pl.BlockSpec(memory_space=where.get(i, pltpu.VMEM)) for i in range(len(args))
            ],
            out_specs=[
                pl.BlockSpec(memory_space=pltpu.HBM if i in far else pltpu.VMEM)
                for i in range(len(outs))
            ],
            scratch_shapes=list(scratch),
            compiler_params=pltpu.CompilerParams(vmem_limit_bytes=16 * 1024 * 1024),
            cost_estimate=cost and pl.CostEstimate(flops=cost[0], bytes_accessed=cost[1], transcendentals=0),
            input_output_aliases=aliases or {},
        )(*args)

    return run


def pack_kernel(q_ref, k_ref, v_ref, g_ref, decay_ref, out_ref, decay_buf, sems, decay_sem):
    fetch = pltpu.make_async_copy(decay_ref, decay_buf, decay_sem)
    fetch.start()
    copies = [
        [
            pltpu.make_async_copy(
                ref.at[:, h * KD : (h + 1) * KD],
                out_ref.at[h, n * TOK : (n + 1) * TOK, :],
                sems.at[h, n],
            )
            for n, ref in enumerate((q_ref, k_ref, v_ref, g_ref))
        ]
        for h in range(HEADS)
    ]
    for copy in sum(copies, []):
        copy.start()
    fetch.wait()
    row = lax.broadcasted_iota(jnp.int32, (16, 256), 0)
    for h in range(HEADS):
        decay = decay_buf[h : h + 1, :]
        high = decay.astype(BF16).astype(F32)
        rest = decay - high
        middle = rest.astype(BF16).astype(F32)
        low = rest - middle
        first = jnp.concatenate([high, middle], axis=1)
        second = jnp.concatenate([low, jnp.zeros_like(low)], axis=1)
        pieces = jnp.where(row == 0, first, jnp.where(row == 1, second, 0.0))
        out_ref[h, 4 * TOK :, :] = pieces.astype(BF16)
    for copy in sum(copies, []):
        copy.wait()


def part(ref, c, n):
    per = CHUNK // TOK
    return ref[c * per : (c + 1) * per, n * TOK : (n + 1) * TOK, :].reshape(CHUNK, 256)


def put(ref, c, n, item):
    per = CHUNK // TOK
    item = item.astype(BF16).reshape(per, TOK, 256)
    ref[c * per : (c + 1) * per, n * TOK : (n + 1) * TOK, :] = item


def rows_of(ref, c, n):
    per = CHUNK // TOK
    return ref.at[c * per : (c + 1) * per, n * TOK : (n + 1) * TOK, :]


def send(source, target, sems, c, n):
    copy = pltpu.make_async_copy(rows_of(source, c, n), rows_of(target, c, n), sems.at[n, c])
    copy.start()
    return copy


def chunk_decay(col_ref, row_ref, c):
    column = col_ref[:, c : c + 1]
    line = row_ref[c : c + 1, :]
    return column, line, line[:, CHUNK - 1 :]


def chunk_weight(column, line):
    t = lax.broadcasted_iota(jnp.int32, (CHUNK, CHUNK), 0)
    s = lax.broadcasted_iota(jnp.int32, (CHUNK, CHUNK), 1)
    return jnp.where(t >= s, jnp.exp(jnp.minimum(column - line, 0.0)), 0.0)


def state_kernel(got_ref, total_ref, states_ref, col_ref, row_ref, decay_ref):
    decay_ref[...] = jnp.zeros_like(decay_ref)
    for i in range(GROUP):
        pieces = got_ref[i, 4 * TOK :, :].astype(F32)
        c, j = divmod(i * TOK, CHUNK)
        for n, piece in enumerate((pieces[0:1, :TOK], pieces[0:1, TOK:], pieces[1:2, :TOK])):
            decay_ref[8 * n + c : 8 * n + c + 1, j : j + TOK] = piece
    pieces = decay_ref[...].astype(BF16)
    t = lax.broadcasted_iota(jnp.int32, (CHUNK, CHUNK), 0)
    s = lax.broadcasted_iota(jnp.int32, (CHUNK, CHUNK), 1)
    lower = (t >= s).astype(F32).astype(BF16)
    lines = nt(pieces, lower)
    row_ref[...] = (lines[0:8] + lines[8:16]) + lines[16:24]
    columns = nt(lower, pieces)
    col_ref[...] = (columns[:, 0:8] + columns[:, 8:16]) + columns[:, 16:24]
    carried = jnp.zeros((KD, VD), F32)
    for c in range(CHUNKS):
        states_ref[c] = carried
        column, line, last = chunk_decay(col_ref, row_ref, c)
        key_tail = (part(got_ref, c, 1).astype(F32) * jnp.exp(last - column)).astype(BF16)
        carried = jnp.exp(last) * carried + tn(key_tail, part(got_ref, c, 2))
    total_ref[...] = carried.astype(BF16)


def local_kernel(got_ref, states_ref, col_ref, row_ref, retained_ref, output_ref):
    for c in range(CHUNKS):
        column, line, last = chunk_decay(col_ref, row_ref, c)
        q = part(got_ref, c, 0)
        scores = nt(q, part(got_ref, c, 1))
        retained = (scores * (SCALE * chunk_weight(column, line))).astype(BF16)
        retained_ref[c] = retained
        output = nn(retained, part(got_ref, c, 2))
        if c:
            tail = (q.astype(F32) * (SCALE * jnp.exp(column))).astype(BF16)
            output = output + nn(tail, states_ref[c].astype(BF16))
        output_ref[c] = output


def output_kernel(
    where_ref, got_ref, states_ref, retained_ref, output_ref, middle_ref, col_ref, row_ref, gain_ref,
    out_ref, total_ref, gain_part_ref, back_ref, total_buf, block_grads, keys_acc, values_acc, sems,
):
    copies = []
    gain = gain_ref[0:1, :]
    middle = jnp.where(where_ref[0] > 0, middle_ref[...].astype(F32), 0.0)
    middle_low = middle.astype(BF16)
    before = jnp.zeros((1, 1), F32)
    gain_part = jnp.zeros((1, VD), F32)
    for c in range(CHUNKS):
        column, line, last = chunk_decay(col_ref, row_ref, c)
        q, k, v = part(got_ref, c, 0), part(got_ref, c, 1), part(got_ref, c, 2)
        from_start = SCALE * jnp.exp(column)
        tail = (q.astype(F32) * from_start).astype(BF16)
        state_in = (states_ref[c] + jnp.exp(before) * middle).astype(BF16)
        output = output_ref[c] + jnp.exp(before) * nn(tail, middle_low)
        before = before + last
        centred = output - jnp.mean(output, axis=1, keepdims=True)
        inverse = lax.rsqrt(jnp.mean(centred * centred, axis=1, keepdims=True) + EPSILON)
        normed = centred * inverse
        wide = part(got_ref, c, 3).astype(F32)
        gain_part = gain_part + jnp.sum(wide * normed, axis=0, keepdims=True)
        scaled = wide * gain
        grad = inverse * (
            scaled
            - jnp.mean(scaled, axis=1, keepdims=True)
            - normed * jnp.mean(scaled * normed, axis=1, keepdims=True)
        )
        grad = grad.astype(BF16)
        block_grads[c] = tn(tail, grad)
        scores = nt(grad, v)
        grad_retained = (scores * (SCALE * chunk_weight(column, line))).astype(BF16)
        queries = nn(grad_retained, k) + from_start * nt(grad, state_in)
        put(back_ref, c, 0, queries)
        copies.append(send(back_ref, out_ref, sems, c, 0))
        keys_acc[c] = tn(grad_retained, q)
        values_acc[c] = tn(retained_ref[c], grad)
    carried = jnp.zeros((KD, VD), F32)
    for c in reversed(range(CHUNKS)):
        column, _, last = chunk_decay(col_ref, row_ref, c)
        keys, values = keys_acc[c], values_acc[c]
        if c < CHUNKS - 1:
            to_end = jnp.exp(last - column)
            after = carried.astype(BF16)
            keys = keys + to_end * nt(part(got_ref, c, 2), after)
            values = values + to_end * nn(part(got_ref, c, 1), after)
        put(back_ref, c, 1, keys)
        put(back_ref, c, 2, values)
        copies.append(send(back_ref, out_ref, sems, c, 1))
        copies.append(send(back_ref, out_ref, sems, c, 2))
        carried = jnp.exp(last) * carried + block_grads[c]
    total_buf[...] = carried.astype(BF16)
    copies.append(pltpu.make_async_copy(total_buf, total_ref, sems.at[3, 0]))
    copies[-1].start()
    gain_part_ref[...] = jnp.zeros_like(gain_part_ref)
    gain_part_ref[0:1, :] = gain_part[:, :128]
    gain_part_ref[1:2, :] = gain_part[:, 128:]
    for copy in copies:
        copy.wait()


def spread_kernel(gain_ref, out_ref):
    for i in range(out_ref.shape[0]):
        out_ref[i] = gain_ref[...]


def fold_kernel(gains_ref, out_ref):
    for h in range(HEADS):
        for j in range(2):
            both = gains_ref[h, j : j + 1, :] + gains_ref[h + GROUP, j : j + 1, :]
            out_ref[2 * h + j : 2 * h + j + 1, :] = both


def last_kernel(where_ref, got_ref, back_ref, middle_ref, col_ref, row_ref, out_ref, buf, sems, out_sems):
    fetches = {}
    for c in reversed(range(CHUNKS)):
        for n in (1, 2):
            fetches[c, n] = send(back_ref, buf, sems, c, n)
    middle = jnp.where(where_ref[0] > 0, 0.0, middle_ref[...].astype(F32)).astype(BF16)
    after = jnp.zeros((1, 1), F32)
    copies = []
    for c in reversed(range(CHUNKS)):
        column, line, last = chunk_decay(col_ref, row_ref, c)
        to_end = jnp.exp(after + (last - column))
        after = after + last
        keys = to_end * nt(part(got_ref, c, 2), middle)
        values = to_end * nn(part(got_ref, c, 1), middle)
        for n, item in ((1, keys), (2, values)):
            fetches[c, n].wait()
            put(buf, c, n, part(buf, c, n).astype(F32) + item)
            copies.append(send(buf, out_ref, out_sems, c, n))
    for copy in copies:
        copy.wait()


def unpack_kernel(got_ref, queries_ref, keys_ref, values_ref, sems):
    copies = []
    for n, ref in enumerate((queries_ref, keys_ref, values_ref)):
        for h in range(HEADS):
            copies.append(
                pltpu.make_async_copy(
                    got_ref.at[h, n * TOK : (n + 1) * TOK, :],
                    ref.at[:, h * KD : (h + 1) * KD],
                    sems.at[n * HEADS + h],
                )
            )
    for copy in copies:
        copy.start()
    for copy in copies:
        copy.wait()


def shards(queries, key_vectors, values, grad_out, log_decay, norm_gain):
    place = lax.axis_index("ctx")
    blocks = lax.axis_size("ctx")
    halves = [list(range(GROUP)), list(range(GROUP, 2 * GROUP))]
    size = lax.axis_size("dp")
    swap = [(i, i ^ GROUP) for i in range(blocks)]
    square = (CHUNKS, CHUNK, 256)

    packed = call(
        pack_kernel,
        [((GROUP, ROWS, 256), BF16)],
        [
            pltpu.VMEM((HEADS, TOK), F32),
            pltpu.SemaphoreType.DMA((HEADS, 4)),
            pltpu.SemaphoreType.DMA,
        ],
        places={i: pltpu.HBM for i in range(5)},
    )(queries[0], key_vectors[0], values[0], grad_out[0], log_decay[0])[0]
    got = lax.all_to_all(packed, "ctx", 0, 0, axis_index_groups=halves, tiled=True)
    where = (place // GROUP).astype(jnp.int32).reshape(1)
    gain = lax.dynamic_slice_in_dim(norm_gain.reshape(HEADS, VD), place % GROUP, 1, 0)
    total, states, column, line = call(
        state_kernel,
        [((KD, VD), BF16), ((CHUNKS, KD, VD), F32), ((CHUNK, 8), F32), ((8, CHUNK), F32)],
        [pltpu.VMEM((32, CHUNK), F32)],
    )(got)
    middle = lax.ppermute(total, "ctx", swap)
    retained, output = call(local_kernel, [(square, BF16), (square, F32)])(
        got, states, column, line
    )
    back, total_grad, gain_part = call(
        output_kernel,
        [((GROUP, BACK, 256), BF16), ((KD, VD), BF16), ((8, 128), F32)],
        [
            pltpu.VMEM((GROUP, BACK, 256), BF16),
            pltpu.VMEM((KD, VD), BF16),
            *[pltpu.VMEM((CHUNKS, 256, 256), F32)] * 3,
            pltpu.SemaphoreType.DMA((4, CHUNKS)),
        ],
        places={0: pltpu.SMEM},
        far=(0, 1),
    )(where, got, states, retained, output, middle, column, line, gain)
    middle_grad = lax.ppermute(total_grad, "ctx", swap)
    gains = lax.all_to_all(
        call(spread_kernel, [((blocks, 8, 128), F32)], cost=(4 * 10**9, 2**20))(gain_part)[0],
        "ctx", 0, 0, tiled=True,
    )
    back = call(
        last_kernel,
        [((GROUP, BACK, 256), BF16)],
        [pltpu.VMEM((GROUP, BACK, 256), BF16), *[pltpu.SemaphoreType.DMA((3, CHUNKS))] * 2],
        places={0: pltpu.SMEM, 2: pltpu.HBM},
        far=(0,),
        aliases={2: 0},
    )(where, got, back, middle_grad, column, line)[0]
    back = lax.all_to_all(back, "ctx", 0, 0, axis_index_groups=halves, tiled=True)
    gain_all = lax.all_gather(call(fold_kernel, [((2 * HEADS, 128), F32)])(gains)[0], "dp")
    results = call(
        unpack_kernel,
        [((TOK, HEADS * KD), BF16)] * 3,
        [pltpu.SemaphoreType.DMA((3 * HEADS,))],
        places={0: pl.ANY},
        far=(0, 1, 2),
    )(back)
    grad_gain = (jnp.sum(gain_all, axis=0) / size).reshape(HEADS * VD)
    return (*(item[None] for item in results), grad_gain)


def solution(mesh):
    return jax.shard_map(
        shards,
        mesh=mesh,
        in_specs=(
            P("dp", "ctx", None),
            P("dp", "ctx", None),
            P("dp", "ctx", None),
            P("dp", "ctx", None),
            P("dp", None, "ctx"),
            P(),
        ),
        out_specs=(P("dp", "ctx", None), P("dp", "ctx", None), P("dp", "ctx", None), P()),
        check_vma=False,
    )
```

```python
import jax
import jax.numpy as jnp
from jax import lax
from jax.experimental import pallas as pl
from jax.experimental.pallas import tpu as pltpu
from jax.sharding import PartitionSpec as P

HEADS = 8
KD = 256
VD = 256
EPSILON = 1e-05

TOK = 128
GROUP = 8
CHUNK = 256
CHUNKS = GROUP * TOK // CHUNK
ROWS = 4 * TOK + 16
BACK = 3 * TOK

F32 = jnp.float32
BF16 = jnp.bfloat16
SCALE = KD ** (-0.5)


def nn(a, b):
    return lax.dot_general(a, b, (((1,), (0,)), ((), ())), preferred_element_type=F32)


def nt(a, b):
    return lax.dot_general(a, b, (((1,), (1,)), ((), ())), preferred_element_type=F32)


def tn(a, b):
    return lax.dot_general(a, b, (((0,), (0,)), ((), ())), preferred_element_type=F32)


def call(kernel, outs, scratch=(), places=None, far=(), cost=None, aliases=None):
    def run(*args):
        where = places or {}
        args = [
            pltpu.with_memory_space_constraint(item, pltpu.HBM) if where.get(i) == pltpu.HBM else item
            for i, item in enumerate(args)
        ]
        return pl.pallas_call(
            kernel,
            out_shape=[
                (pltpu.HBM if i in far else jax.ShapeDtypeStruct)(shape, kind)
                for i, (shape, kind) in enumerate(outs)
            ],
            in_specs=[
                pl.BlockSpec(memory_space=where.get(i, pltpu.VMEM)) for i in range(len(args))
            ],
            out_specs=[
                pl.BlockSpec(memory_space=pltpu.HBM if i in far else pltpu.VMEM)
                for i in range(len(outs))
            ],
            scratch_shapes=list(scratch),
            compiler_params=pltpu.CompilerParams(vmem_limit_bytes=16 * 1024 * 1024),
            cost_estimate=cost and pl.CostEstimate(flops=cost[0], bytes_accessed=cost[1], transcendentals=0),
            input_output_aliases=aliases or {},
        )(*args)

    return run


def pack_kernel(q_ref, k_ref, v_ref, g_ref, decay_ref, out_ref, decay_buf, sems, decay_sem):
    fetch = pltpu.make_async_copy(decay_ref, decay_buf, decay_sem)
    fetch.start()
    copies = [
        [
            pltpu.make_async_copy(
                ref.at[:, h * KD : (h + 1) * KD],
                out_ref.at[h, n * TOK : (n + 1) * TOK, :],
                sems.at[h, n],
            )
            for n, ref in enumerate((q_ref, k_ref, v_ref, g_ref))
        ]
        for h in range(HEADS)
    ]
    for copy in sum(copies, []):
        copy.start()
    fetch.wait()
    row = lax.broadcasted_iota(jnp.int32, (16, 256), 0)
    for h in range(HEADS):
        decay = decay_buf[h : h + 1, :]
        high = decay.astype(BF16).astype(F32)
        rest = decay - high
        middle = rest.astype(BF16).astype(F32)
        low = rest - middle
        first = jnp.concatenate([high, middle], axis=1)
        second = jnp.concatenate([low, jnp.zeros_like(low)], axis=1)
        pieces = jnp.where(row == 0, first, jnp.where(row == 1, second, 0.0))
        out_ref[h, 4 * TOK :, :] = pieces.astype(BF16)
    for copy in sum(copies, []):
        copy.wait()


def part(ref, c, n):
    per = CHUNK // TOK
    return ref[c * per : (c + 1) * per, n * TOK : (n + 1) * TOK, :].reshape(CHUNK, 256)


def put(ref, c, n, item):
    per = CHUNK // TOK
    item = item.astype(BF16).reshape(per, TOK, 256)
    ref[c * per : (c + 1) * per, n * TOK : (n + 1) * TOK, :] = item


def rows_of(ref, c, n):
    per = CHUNK // TOK
    return ref.at[c * per : (c + 1) * per, n * TOK : (n + 1) * TOK, :]


def send(source, target, sems, c, n):
    copy = pltpu.make_async_copy(rows_of(source, c, n), rows_of(target, c, n), sems.at[n, c])
    copy.start()
    return copy


def chunk_decay(col_ref, row_ref, c):
    column = col_ref[:, c : c + 1]
    line = row_ref[c : c + 1, :]
    return column, line, line[:, CHUNK - 1 :]


def chunk_weight(column, line):
    t = lax.broadcasted_iota(jnp.int32, (CHUNK, CHUNK), 0)
    s = lax.broadcasted_iota(jnp.int32, (CHUNK, CHUNK), 1)
    return jnp.where(t >= s, jnp.exp(jnp.minimum(column - line, 0.0)), 0.0)


def state_kernel(got_ref, total_ref, states_ref, col_ref, row_ref, decay_ref):
    decay_ref[...] = jnp.zeros_like(decay_ref)
    for i in range(GROUP):
        pieces = got_ref[i, 4 * TOK :, :].astype(F32)
        c, j = divmod(i * TOK, CHUNK)
        for n, piece in enumerate((pieces[0:1, :TOK], pieces[0:1, TOK:], pieces[1:2, :TOK])):
            decay_ref[8 * n + c : 8 * n + c + 1, j : j + TOK] = piece
    pieces = decay_ref[...].astype(BF16)
    t = lax.broadcasted_iota(jnp.int32, (CHUNK, CHUNK), 0)
    s = lax.broadcasted_iota(jnp.int32, (CHUNK, CHUNK), 1)
    lower = (t >= s).astype(F32).astype(BF16)
    lines = nt(pieces, lower)
    row_ref[...] = (lines[0:8] + lines[8:16]) + lines[16:24]
    columns = nt(lower, pieces)
    col_ref[...] = (columns[:, 0:8] + columns[:, 8:16]) + columns[:, 16:24]
    carried = jnp.zeros((KD, VD), F32)
    for c in range(CHUNKS):
        states_ref[c] = carried
        column, line, last = chunk_decay(col_ref, row_ref, c)
        key_tail = (part(got_ref, c, 1).astype(F32) * jnp.exp(last - column)).astype(BF16)
        carried = jnp.exp(last) * carried + tn(key_tail, part(got_ref, c, 2))
    total_ref[...] = carried.astype(BF16)


def local_kernel(got_ref, states_ref, col_ref, row_ref, retained_ref, output_ref):
    for c in range(CHUNKS):
        column, line, last = chunk_decay(col_ref, row_ref, c)
        q = part(got_ref, c, 0)
        scores = nt(q, part(got_ref, c, 1))
        retained = (scores * (SCALE * chunk_weight(column, line))).astype(BF16)
        retained_ref[c] = retained
        output = nn(retained, part(got_ref, c, 2))
        if c:
            tail = (q.astype(F32) * (SCALE * jnp.exp(column))).astype(BF16)
            output = output + nn(tail, states_ref[c].astype(BF16))
        output_ref[c] = output


def output_kernel(
    where_ref, got_ref, states_ref, retained_ref, output_ref, middle_ref, col_ref, row_ref, gain_ref,
    out_ref, total_ref, gain_part_ref, back_ref, total_buf, block_grads, keys_acc, values_acc, sems,
):
    copies = []
    gain = gain_ref[0:1, :]
    middle = jnp.where(where_ref[0] > 0, middle_ref[...].astype(F32), 0.0)
    middle_low = middle.astype(BF16)
    before = jnp.zeros((1, 1), F32)
    gain_part = jnp.zeros((1, VD), F32)
    for c in range(CHUNKS):
        column, line, last = chunk_decay(col_ref, row_ref, c)
        q, k, v = part(got_ref, c, 0), part(got_ref, c, 1), part(got_ref, c, 2)
        from_start = SCALE * jnp.exp(column)
        tail = (q.astype(F32) * from_start).astype(BF16)
        state_in = (states_ref[c] + jnp.exp(before) * middle).astype(BF16)
        output = output_ref[c] + jnp.exp(before) * nn(tail, middle_low)
        before = before + last
        centred = output - jnp.mean(output, axis=1, keepdims=True)
        inverse = lax.rsqrt(jnp.mean(centred * centred, axis=1, keepdims=True) + EPSILON)
        normed = centred * inverse
        wide = part(got_ref, c, 3).astype(F32)
        gain_part = gain_part + jnp.sum(wide * normed, axis=0, keepdims=True)
        scaled = wide * gain
        grad = inverse * (
            scaled
            - jnp.mean(scaled, axis=1, keepdims=True)
            - normed * jnp.mean(scaled * normed, axis=1, keepdims=True)
        )
        grad = grad.astype(BF16)
        block_grads[c] = tn(tail, grad)
        scores = nt(grad, v)
        grad_retained = (scores * (SCALE * chunk_weight(column, line))).astype(BF16)
        queries = nn(grad_retained, k) + from_start * nt(grad, state_in)
        put(back_ref, c, 0, queries)
        copies.append(send(back_ref, out_ref, sems, c, 0))
        keys_acc[c] = tn(grad_retained, q)
        values_acc[c] = tn(retained_ref[c], grad)
    carried = jnp.zeros((KD, VD), F32)
    for c in reversed(range(CHUNKS)):
        column, _, last = chunk_decay(col_ref, row_ref, c)
        keys, values = keys_acc[c], values_acc[c]
        if c < CHUNKS - 1:
            to_end = jnp.exp(last - column)
            after = carried.astype(BF16)
            keys = keys + to_end * nt(part(got_ref, c, 2), after)
            values = values + to_end * nn(part(got_ref, c, 1), after)
        put(back_ref, c, 1, keys)
        put(back_ref, c, 2, values)
        copies.append(send(back_ref, out_ref, sems, c, 1))
        copies.append(send(back_ref, out_ref, sems, c, 2))
        carried = jnp.exp(last) * carried + block_grads[c]
    total_buf[...] = carried.astype(BF16)
    copies.append(pltpu.make_async_copy(total_buf, total_ref, sems.at[3, 0]))
    copies[-1].start()
    gain_part_ref[...] = jnp.zeros_like(gain_part_ref)
    gain_part_ref[0:1, :] = gain_part[:, :128]
    gain_part_ref[1:2, :] = gain_part[:, 128:]
    for copy in copies:
        copy.wait()


def spread_kernel(gain_ref, out_ref):
    for i in range(out_ref.shape[0]):
        out_ref[i] = gain_ref[...]


def fold_kernel(gains_ref, out_ref):
    for h in range(HEADS):
        for j in range(2):
            both = gains_ref[h, j : j + 1, :] + gains_ref[h + GROUP, j : j + 1, :]
            out_ref[2 * h + j : 2 * h + j + 1, :] = both


def last_kernel(where_ref, got_ref, back_ref, middle_ref, col_ref, row_ref, out_ref, buf, sems, out_sems):
    fetches = {}
    for c in reversed(range(CHUNKS)):
        for n in (1, 2):
            fetches[c, n] = send(back_ref, buf, sems, c, n)
    middle = jnp.where(where_ref[0] > 0, 0.0, middle_ref[...].astype(F32)).astype(BF16)
    after = jnp.zeros((1, 1), F32)
    copies = []
    for c in reversed(range(CHUNKS)):
        column, line, last = chunk_decay(col_ref, row_ref, c)
        to_end = jnp.exp(after + (last - column))
        after = after + last
        keys = to_end * nt(part(got_ref, c, 2), middle)
        values = to_end * nn(part(got_ref, c, 1), middle)
        for n, item in ((1, keys), (2, values)):
            fetches[c, n].wait()
            put(buf, c, n, part(buf, c, n).astype(F32) + item)
            copies.append(send(buf, out_ref, out_sems, c, n))
    for copy in copies:
        copy.wait()


def unpack_kernel(got_ref, gains_ref, queries_ref, keys_ref, values_ref, gain_ref, sems):
    copies = []
    for n, ref in enumerate((queries_ref, keys_ref, values_ref)):
        for h in range(HEADS):
            copies.append(
                pltpu.make_async_copy(
                    got_ref.at[h, n * TOK : (n + 1) * TOK, :],
                    ref.at[:, h * KD : (h + 1) * KD],
                    sems.at[n * HEADS + h],
                )
            )
    for copy in copies:
        copy.start()
    gain = gains_ref[0]
    for i in range(1, gains_ref.shape[0]):
        gain = gain + gains_ref[i]
    gain_ref[...] = gain / gains_ref.shape[0]
    for copy in copies:
        copy.wait()


def shards(queries, key_vectors, values, grad_out, log_decay, norm_gain):
    place = lax.axis_index("ctx")
    blocks = lax.axis_size("ctx")
    halves = [list(range(GROUP)), list(range(GROUP, 2 * GROUP))]
    swap = [(i, i ^ GROUP) for i in range(blocks)]
    square = (CHUNKS, CHUNK, 256)

    packed = call(
        pack_kernel,
        [((GROUP, ROWS, 256), BF16)],
        [
            pltpu.VMEM((HEADS, TOK), F32),
            pltpu.SemaphoreType.DMA((HEADS, 4)),
            pltpu.SemaphoreType.DMA,
        ],
        places={i: pltpu.HBM for i in range(5)},
    )(queries[0], key_vectors[0], values[0], grad_out[0], log_decay[0])[0]
    got = lax.all_to_all(packed, "ctx", 0, 0, axis_index_groups=halves, tiled=True)
    where = (place // GROUP).astype(jnp.int32).reshape(1)
    gain = lax.dynamic_slice_in_dim(norm_gain.reshape(HEADS, VD), place % GROUP, 1, 0)
    total, states, column, line = call(
        state_kernel,
        [((KD, VD), BF16), ((CHUNKS, KD, VD), F32), ((CHUNK, 8), F32), ((8, CHUNK), F32)],
        [pltpu.VMEM((32, CHUNK), F32)],
    )(got)
    middle = lax.ppermute(total, "ctx", swap)
    retained, output = call(local_kernel, [(square, BF16), (square, F32)])(
        got, states, column, line
    )
    back, total_grad, gain_part = call(
        output_kernel,
        [((GROUP, BACK, 256), BF16), ((KD, VD), BF16), ((8, 128), F32)],
        [
            pltpu.VMEM((GROUP, BACK, 256), BF16),
            pltpu.VMEM((KD, VD), BF16),
            *[pltpu.VMEM((CHUNKS, 256, 256), F32)] * 3,
            pltpu.SemaphoreType.DMA((4, CHUNKS)),
        ],
        places={0: pltpu.SMEM},
        far=(0, 1),
    )(where, got, states, retained, output, middle, column, line, gain)
    middle_grad = lax.ppermute(total_grad, "ctx", swap)
    gains = lax.all_to_all(
        call(spread_kernel, [((blocks, 8, 128), F32)], cost=(4 * 10**9, 2**20))(gain_part)[0],
        "ctx", 0, 0, tiled=True,
    )
    back = call(
        last_kernel,
        [((GROUP, BACK, 256), BF16)],
        [pltpu.VMEM((GROUP, BACK, 256), BF16), *[pltpu.SemaphoreType.DMA((3, CHUNKS))] * 2],
        places={0: pltpu.SMEM, 2: pltpu.HBM},
        far=(0,),
        aliases={2: 0},
    )(where, got, back, middle_grad, column, line)[0]
    back = lax.all_to_all(back, "ctx", 0, 0, axis_index_groups=halves, tiled=True)
    gain_all = lax.all_gather(call(fold_kernel, [((2 * HEADS, 128), F32)])(gains)[0], "dp")
    *results, grad_gain = call(
        unpack_kernel,
        [*[((TOK, HEADS * KD), BF16)] * 3, ((2 * HEADS, 128), F32)],
        [pltpu.SemaphoreType.DMA((3 * HEADS,))],
        places={0: pl.ANY},
        far=(0, 1, 2),
    )(back, gain_all)
    return (*(item[None] for item in results), grad_gain.reshape(HEADS * VD))


def solution(mesh):
    return jax.shard_map(
        shards,
        mesh=mesh,
        in_specs=(
            P("dp", "ctx", None),
            P("dp", "ctx", None),
            P("dp", "ctx", None),
            P("dp", "ctx", None),
            P("dp", None, "ctx"),
            P(),
        ),
        out_specs=(P("dp", "ctx", None), P("dp", "ctx", None), P("dp", "ctx", None), P()),
        check_vma=False,
    )
```
